512 devices in a mesh: row: 16 (over y, x), col: 32 (over z, core).
Axes of the slice: x: 4, y: 4, z: 16, core: 2. Of those that a mesh axis runs over, the one named last changes fastest.
Arguments:
- hidden: bfloat16 [512, 16384], P('col', 'row'), may hold values from -6 to 6
- cotangent: bfloat16 [512, 16384], P('col', 'row'), may hold values from -6 to 6
- importance: bfloat16 [512], P('col'), may hold values from 0.099609375 to 10
- positions: int32 [512], P('col'), may hold values from 0 to 4606, as said below
- segments: int32 [512], P('col'), may hold values from 0 to 3, as said below
- norm_gain: bfloat16 [16384], P('row'), may hold values from 0.5 to 1.5
- query_weight_matrix: bfloat16 [16384, 16384], P('row', 'col')
- key_weight: bfloat16 [16384, 1024], P('row', 'col')
- value_weight_matrix: bfloat16 [16384, 1024], P('row', 'col'), may hold values from -0.046875 to 0.046875
- output_weight_matrix: bfloat16 [16384, 16384], P('col', 'row'), may hold values from -0.046875 to 0.046875
- query_down_factor: bfloat16 [16384, 64], P('row'), may hold values from -0.046875 to 0.046875
- query_up_factor: bfloat16 [64, 16384], P(None, 'col'), may hold values from -0.75 to 0.75
- output_down_factor: bfloat16 [16384, 64], P('col'), may hold values from -0.046875 to 0.046875
- out_up: bfloat16 [64, 16384], P(None, 'row'), may hold values from -0.75 to 0.75
Outputs:
- input_grad: float32 [512, 16384], P('col', 'row')
- query_down_gradient: float32 [16384, 64], P('row')
- query_up_gradient: float32 [64, 16384], P(None, 'col')
- output_down_gradient: float32 [16384, 64], P('col')
- output_up_gradient: float32 [64, 16384], P(None, 'row')
The draws below stay inside these ranges and needn't reach their ends.
Inputs may be any that keep to these rules, and one draw needn't show every extreme that they name: `segments`: rollout numbers never fall along the tokens, and each of the 4 rollouts holds at least one token. positions rise by one from token to token within a rollout.
All inputs are finite; a program needn't handle non-finite values.
Results may differ from the reference program's by a relative error of at most 0.012.
The reference program's roundings to bfloat16 on the way count: a program that leaves them out, or rounds other values in their place, can miss the bound.
Values may be sent and summed in bfloat16 or wider, within the bound.
A program may use at most 64 MiB of HBM per device.

```python
import math
import jax
import jax.numpy as jnp
from jax import lax

MODEL_WIDTH = 16384
QUERY_HEADS = 128
KEY_VALUE_HEADS = 8
HEAD_SIZE = 128
RANK = 64
ROLLOUTS = 4
BATCH_TOKENS = 512


def rollout_cuts(key):
    shuffled = jax.random.permutation(key, BATCH_TOKENS - 1)
    return jnp.sort(shuffled[:ROLLOUTS - 1] + 1).astype(jnp.int32)


def rollout_index(cuts):
    token_index = jnp.arange(BATCH_TOKENS, dtype=jnp.int32)
    return jnp.sum((token_index[:, None] >= cuts[None, :]).astype(jnp.int32), axis=1)


def key_base(key):
    return jax.random.normal(key, (MODEL_WIDTH, KEY_VALUE_HEADS * HEAD_SIZE), jnp.float32) / math.sqrt(MODEL_WIDTH)


def draw_segments(key, part):
    cuts = rollout_cuts(key)
    return rollout_index(cuts)


def draw_positions(key, part):
    cuts = rollout_cuts(key)
    key = jax.random.fold_in(key, 2)
    rollout_ids = rollout_index(cuts)
    offsets = jax.random.randint(key, (ROLLOUTS,), 0, 4096, dtype=jnp.int32)
    offsets = offsets.at[0].set(0)
    offsets = offsets.at[ROLLOUTS - 1].set(4095 + cuts[ROLLOUTS - 2])
    starts = jnp.concatenate([jnp.zeros((1,), jnp.int32), cuts])
    token_index = jnp.arange(BATCH_TOKENS, dtype=jnp.int32)
    return (offsets[rollout_ids] + token_index - starts[rollout_ids]).astype(jnp.int32)


def draw_key_weight(key, part):
    shared_terms = key_base(key)
    return shared_terms.astype(jnp.bfloat16)


def draw_query_weight_matrix(key, part):
    key = jax.random.fold_in(key, 4)
    weight = jax.random.normal(key, (MODEL_WIDTH, QUERY_HEADS * HEAD_SIZE), jnp.float32) / math.sqrt(MODEL_WIDTH)
    return weight.astype(jnp.bfloat16)


def level_of(stream_key, shape, split, least, high):
    level = 1.0
    for position, parts in split:
        heights = jax.random.uniform(jax.random.fold_in(jax.random.fold_in(stream_key, 6), position), (parts,), jnp.float32, least / len(split), high / len(split))
        level = level * jnp.repeat(jnp.exp(heights), shape[position] // parts).reshape((-1,) + (1,) * (len(shape) - 1 - position))
    return level


def scatter_about(rng, extent, scale, most, split=(), held_as=jnp.bfloat16):
    drawn = scale * jax.random.normal(rng, extent, jnp.float32)
    if split:
        drawn = drawn * level_of(rng, extent, split, -0.22, 0.18)
    return jnp.clip(drawn, -most, most).astype(held_as)


def setup_inputs(seed: int = 0) -> dict:
    keys = jax.random.split(jax.random.key(seed), 15)
    hidden = scatter_about(keys[0], (BATCH_TOKENS, MODEL_WIDTH), 1.0, 6.0, ((0, 32), (1, 16)))
    cotangent = scatter_about(keys[1], (BATCH_TOKENS, MODEL_WIDTH), 1.0, 6.0, ((0, 32), (1, 16)))
    importance = jnp.clip(jnp.exp(math.log(10.0) - 4.609084 * jax.random.uniform(keys[2], (BATCH_TOKENS,), jnp.float32) ** level_of(keys[2], (BATCH_TOKENS,), ((0, 32),), -0.2, 0.2)), 0.099609375, 10.0).astype(jnp.bfloat16)
    positions = draw_positions(jax.random.fold_in(keys[14], 71), 0)
    segments = draw_segments(jax.random.fold_in(keys[14], 71), 0)
    norm_gain = jnp.clip(1.0 + 0.1 * jax.random.normal(keys[5], (MODEL_WIDTH,), jnp.float32), 0.5, 1.5).astype(jnp.bfloat16)
    query_weight_matrix = draw_query_weight_matrix(jax.random.fold_in(keys[14], 71), 0)
    key_weight = draw_key_weight(jax.random.fold_in(keys[14], 71), 0)
    value_weight_matrix = scatter_about(keys[8], (MODEL_WIDTH, KEY_VALUE_HEADS * HEAD_SIZE), MODEL_WIDTH ** -0.5, 0.046875, ((0, 16), (1, 32)))
    output_weight_matrix = scatter_about(keys[9], (QUERY_HEADS * HEAD_SIZE, MODEL_WIDTH), (QUERY_HEADS * HEAD_SIZE) ** -0.5, 0.046875, ((0, 32), (1, 16)))
    query_down_factor = scatter_about(keys[10], (MODEL_WIDTH, RANK), MODEL_WIDTH ** -0.5, 0.046875, ((0, 16),))
    query_up_factor = scatter_about(keys[11], (RANK, QUERY_HEADS * HEAD_SIZE), RANK ** -0.5, 0.75, ((1, 32),))
    output_down_factor = scatter_about(keys[12], (QUERY_HEADS * HEAD_SIZE, RANK), (QUERY_HEADS * HEAD_SIZE) ** -0.5, 0.046875, ((0, 32),))
    out_up = scatter_about(keys[13], (RANK, MODEL_WIDTH), RANK ** -0.5, 0.75, ((1, 16),))
    return dict(hidden=hidden, cotangent=cotangent, importance=importance, positions=positions, segments=segments, norm_gain=norm_gain, query_weight_matrix=query_weight_matrix, key_weight=key_weight, value_weight_matrix=value_weight_matrix, output_weight_matrix=output_weight_matrix, query_down_factor=query_down_factor, query_up_factor=query_up_factor, output_down_factor=output_down_factor, out_up=out_up)


norm_eps = 1e-05
adapter_scale = 2.0
ratio_cap = 2.0
rope_base = 500000.0
masked_fill = -1e+30

def narrow_precision(tensor):
    return lax.optimization_barrier(tensor.astype(jnp.bfloat16))

def rope_tables(position_ids, head_width):
    half_width = head_width // 2
    frequency = jnp.exp(jnp.arange(half_width, dtype=jnp.float32) * (-2.0 * math.log(rope_base) / head_width))
    angles = position_ids.astype(jnp.float32)[:, None] * frequency[None, :]
    return (jnp.cos(angles)[:, None, :], jnp.sin(angles)[:, None, :])

def apply_rotation(tensor, cosine_lookup, sine_lookup):
    half_width = tensor.shape[-1] // 2
    first_half = tensor[..., :half_width]
    second_half = tensor[..., half_width:]
    return jnp.concatenate([first_half * cosine_lookup - second_half * sine_lookup, second_half * cosine_lookup + first_half * sine_lookup], axis=-1)

def reverse_rotation(tensor, cosine_lookup, sine_lookup):
    half_width = tensor.shape[-1] // 2
    first_half = tensor[..., :half_width]
    second_half = tensor[..., half_width:]
    return jnp.concatenate([first_half * cosine_lookup + second_half * sine_lookup, second_half * cosine_lookup - first_half * sine_lookup], axis=-1)

def reference(hidden, cotangent, importance, positions, segments, norm_gain, query_weight_matrix, key_weight, value_weight_matrix, output_weight_matrix, query_down_factor, query_up_factor, output_down_factor, out_up):
    hidden_wide = hidden.astype(jnp.float32)
    gain_wide = norm_gain.astype(jnp.float32)
    inverse_rms = lax.rsqrt(lax.optimization_barrier(jnp.mean(hidden_wide * hidden_wide, axis=1)) + norm_eps)
    normalized = (hidden_wide * inverse_rms[:, None] * gain_wide[None, :]).astype(jnp.bfloat16)
    reduced_query = jnp.dot(normalized, query_down_factor, preferred_element_type=jnp.float32).astype(jnp.bfloat16)
    query_linear_part = jnp.dot(normalized, query_weight_matrix, preferred_element_type=jnp.float32) + adapter_scale * jnp.dot(reduced_query, query_up_factor, preferred_element_type=jnp.float32)
    key_linear_part = jnp.dot(normalized, key_weight, preferred_element_type=jnp.float32)
    value_row_block = narrow_precision(jnp.dot(normalized, value_weight_matrix, preferred_element_type=jnp.float32)).reshape(BATCH_TOKENS, KEY_VALUE_HEADS, HEAD_SIZE)
    cosine_lookup, sine_lookup = rope_tables(positions, HEAD_SIZE)
    queries = narrow_precision(apply_rotation(query_linear_part.reshape(BATCH_TOKENS, QUERY_HEADS, HEAD_SIZE), cosine_lookup, sine_lookup))
    key_row_block = narrow_precision(apply_rotation(key_linear_part.reshape(BATCH_TOKENS, KEY_VALUE_HEADS, HEAD_SIZE), cosine_lookup, sine_lookup))
    token_index = jnp.arange(BATCH_TOKENS, dtype=jnp.int32)
    allowed = (segments[:, None] == segments[None, :]) & (token_index[None, :] <= token_index[:, None])
    weighted_values = narrow_precision(cotangent.astype(jnp.float32) * jnp.minimum(importance.astype(jnp.float32), ratio_cap)[:, None])
    reduced_gradient = jnp.dot(weighted_values, out_up.T, preferred_element_type=jnp.float32).astype(jnp.bfloat16)
    attention_linear = jnp.dot(weighted_values, output_weight_matrix.T, preferred_element_type=jnp.float32) + adapter_scale * jnp.dot(reduced_gradient, output_down_factor.T, preferred_element_type=jnp.float32)
    attention_grad = narrow_precision(attention_linear).reshape(BATCH_TOKENS, QUERY_HEADS, HEAD_SIZE)
    per_group_share = QUERY_HEADS // KEY_VALUE_HEADS
    score_scale = HEAD_SIZE ** (-0.5)

    def group_sweep(group_index):
        first_head = group_index * per_group_share
        group_queries = lax.dynamic_slice_in_dim(queries, first_head, per_group_share, 1).astype(jnp.float32)
        group_grads = lax.dynamic_slice_in_dim(attention_grad, first_head, per_group_share, 1).astype(jnp.float32)
        group_keys = lax.dynamic_index_in_dim(key_row_block, group_index, 1, keepdims=False).astype(jnp.float32)
        group_values = lax.dynamic_index_in_dim(value_row_block, group_index, 1, keepdims=False).astype(jnp.float32)
        scores = jnp.einsum('qhd,kd->hqk', group_queries, group_keys) * score_scale
        scores = jnp.where(allowed[None], scores, masked_fill)
        shifted = jnp.exp(scores - lax.optimization_barrier(jnp.max(scores, axis=2, keepdims=True)))
        attention_probs = shifted / lax.optimization_barrier(jnp.sum(shifted, axis=2, keepdims=True))
        probs_wide = narrow_precision(attention_probs).astype(jnp.float32)
        attended_rows = jnp.einsum('hqk,kd->qhd', probs_wide, group_values).astype(jnp.bfloat16)
        prob_grad = jnp.einsum('qhd,kd->hqk', group_grads, group_values)
        row_dot = lax.optimization_barrier(jnp.sum(attention_probs * prob_grad, axis=2, keepdims=True))
        score_grad = narrow_precision(attention_probs * (prob_grad - row_dot) * score_scale).astype(jnp.float32)
        query_gradient_rotated = jnp.einsum('hqk,kd->qhd', score_grad, group_keys)
        key_gradient = jnp.einsum('hqk,qhd->kd', score_grad, group_queries)
        value_gradient = jnp.einsum('hqk,qhd->kd', probs_wide, group_grads)
        return (attended_rows, query_gradient_rotated, key_gradient, value_gradient)
    attended_rows, query_gradient_rotated, key_gradient, value_gradient = lax.map(group_sweep, jnp.arange(KEY_VALUE_HEADS, dtype=jnp.int32))
    attended_full = jnp.transpose(attended_rows, (1, 0, 2, 3)).reshape(BATCH_TOKENS, QUERY_HEADS * HEAD_SIZE)
    query_gradient_rotated = jnp.transpose(query_gradient_rotated, (1, 0, 2, 3)).reshape(BATCH_TOKENS, QUERY_HEADS, HEAD_SIZE)
    query_gradient = reverse_rotation(query_gradient_rotated, cosine_lookup, sine_lookup).astype(jnp.bfloat16).reshape(BATCH_TOKENS, QUERY_HEADS * HEAD_SIZE)
    key_gradient = reverse_rotation(jnp.transpose(key_gradient, (1, 0, 2)), cosine_lookup, sine_lookup).reshape(BATCH_TOKENS, KEY_VALUE_HEADS * HEAD_SIZE)
    value_gradient = jnp.transpose(value_gradient, (1, 0, 2)).reshape(BATCH_TOKENS, KEY_VALUE_HEADS * HEAD_SIZE)
    reduced_output = jnp.dot(attended_full, output_down_factor, preferred_element_type=jnp.float32).astype(jnp.bfloat16)
    reduced_backprop = jnp.dot(query_gradient, query_up_factor.T, preferred_element_type=jnp.float32).astype(jnp.bfloat16)
    output_up_gradient = adapter_scale * jnp.dot(reduced_output.T, weighted_values, preferred_element_type=jnp.float32)
    output_down_gradient = adapter_scale * jnp.dot(attended_full.T, reduced_gradient, preferred_element_type=jnp.float32)
    query_up_gradient = adapter_scale * jnp.dot(reduced_query.T, query_gradient, preferred_element_type=jnp.float32)
    query_down_gradient = adapter_scale * jnp.dot(normalized.T, reduced_backprop, preferred_element_type=jnp.float32)
    normalized_gradient = jnp.dot(query_gradient, query_weight_matrix.T, preferred_element_type=jnp.float32) + adapter_scale * jnp.dot(reduced_backprop, query_down_factor.T, preferred_element_type=jnp.float32)
    normalized_gradient = normalized_gradient + jnp.dot(key_gradient, key_weight.astype(jnp.float32).T, precision=lax.Precision.HIGHEST)
    normalized_gradient = normalized_gradient + jnp.dot(value_gradient, value_weight_matrix.astype(jnp.float32).T, precision=lax.Precision.HIGHEST)
    dot_term = lax.optimization_barrier(jnp.sum(hidden_wide * gain_wide[None, :] * normalized_gradient, axis=1))
    input_grad = weighted_values.astype(jnp.float32) + inverse_rms[:, None] * gain_wide[None, :] * normalized_gradient - hidden_wide * (inverse_rms ** 3 * dot_term / MODEL_WIDTH)[:, None]
    return (input_grad, query_down_gradient, query_up_gradient, output_down_gradient, output_up_gradient)
```

```python
import functools
import math

import jax
import jax.numpy as jnp
from jax import lax
from jax.experimental import pallas as pl
from jax.experimental.pallas import tpu as pltpu
from jax.sharding import PartitionSpec as P

MODEL_WIDTH = 16384
HEAD = 128
RANK = 64
GROUP = 4
EPS = 1e-05
CAP = 2.0
BASE = 500000.0
FILL = -1e30
SCALE = HEAD**-0.5
MESH = pl.DeviceIdType.MESH
F32 = jnp.float32
BF16 = jnp.bfloat16
REACH = 4


def nn(a, b):
    return lax.dot_general(a, b, (((1,), (0,)), ((), ())), preferred_element_type=F32)


def nt(a, b):
    return lax.dot_general(a, b, (((1,), (1,)), ((), ())), preferred_element_type=F32)


def tn(a, b):
    return lax.dot_general(a, b, (((0,), (0,)), ((), ())), preferred_element_type=F32)


def remote(src, dst, send, recv, device):
    return pltpu.make_async_remote_copy(
        src_ref=src, dst_ref=dst, send_sem=send, recv_sem=recv,
        device_id=device, device_id_type=MESH,
    )


def kernel(
    R, Z,
    hid, cot, aux_in, gain, wq, qdown, kvt_own, wo, oup, odown, qup,
    igrad, qdown_g, qup_g, odown_g, oup_g,
    h_all, w_all, n_all, aux_all, kvt,
    ssq, part, rx, kvx, kvpart, kvrx, qg_all, kvg_all, att_all, dots,
    own, sib_out, sib_in, hop_out, hop_in, low_all,
    ring_s, ring_r, sib_s, sib_r, ssq_s, ssq_r, aux_s, aux_r, auxsib, kvt_s, kvt_r,
    rs_s, rs_r, kvx_s, kvx_r, kvp_s, kvp_r, qg_s, qg_r, kvg_s, kvg_r, att_s, att_r,
    sg_s, sg_r, hop_s, hop_r, low_s, low_r, lowsib, dot_s, dot_r,
):
    row = lax.axis_index("row")
    col = lax.axis_index("col")
    z = lax.div(col, 2)
    core = lax.rem(col, 2)
    B = hid.shape[0]
    S = 2 * B
    T = S * Z
    D = hid.shape[1]
    H = wo.shape[0]
    heads = H // HEAD
    CH = 4
    counts = {1: Z // 2, -1: Z - 1 - Z // 2}
    dirs = (1, -1)

    def zmod(v):
        return lax.rem(v + 2 * Z, Z)

    def at_z(v):
        return {"col": zmod(v) * 2 + core}

    sibling = {"col": z * 2 + 1 - core}
    pair = z + 1 - 2 * lax.rem(z, 2)

    def peer(k):
        return lax.rem(row + k, R)

    def each(n, f):
        def step(k, carry):
            f(k)
            return carry
        lax.fori_loop(1, n, step, 0)

    def row_copy(src, dst, ss, rs, k):
        return remote(src, dst, ss.at[k], rs, {"row": peer(k)})

    def row_bcast(src, dst_all, ss, rs):
        each(R, lambda k: row_copy(src, dst_all.at[row], ss, rs.at[row], k).start())

    def row_recv(dst_all, rs, ss, k):
        s = peer(k)
        row_copy(dst_all.at[s], dst_all.at[s], ss, rs.at[s], k).wait_recv()

    def row_done(src, dst_all, ss, rs):
        each(R, lambda k: row_copy(src, dst_all.at[row], ss, rs.at[row], k).wait_send())

    barrier = pltpu.get_barrier_semaphore()
    each(R, lambda k: pl.semaphore_signal(
        barrier, inc=1, device_id={"row": peer(k)}, device_id_type=MESH))
    each(Z, lambda k: pl.semaphore_signal(
        barrier, inc=1, device_id=at_z(z + k), device_id_type=MESH))
    pl.semaphore_signal(barrier, inc=1, device_id=sibling, device_id_type=MESH)
    pl.semaphore_signal(
        barrier, inc=1, device_id={"col": pair * 2 + 1 - core}, device_id_type=MESH)

    aux0 = aux_in[...]
    hf = hid[...].astype(F32)
    gf = gain[...].astype(F32)
    w_own = (cot[...].astype(F32) * aux0[:, 6:7]).astype(BF16)
    w_all[z, core] = w_own
    h_all[z, core] = hid[...]
    ssq[row] = jnp.broadcast_to(jnp.sum(hf * hf, axis=1, keepdims=True), (B, 128))
    member = lax.rem(col, GROUP)
    kvt[member] = kvt_own[...]
    pl.semaphore_wait(barrier, R - 1 + Z - 1 + 2)

    arrays = (w_all, h_all)
    started = []

    def ring_send(a, d, ch, t):
        off = t if ch == 0 else (0 if t == 0 else REACH + t)
        block = arrays[a].at[zmod(z - d * off), core]
        target = z + d * (REACH + 1 if ch == 1 and t == 0 else 1)
        i = 0 if d == 1 else 1
        cp = remote(block, block, ring_s.at[a, i, ch, t], ring_r.at[a, i, ch, t], at_z(target))
        cp.start()
        started.append(cp)
        return cp

    sibs = []

    def sib_send(a, i, off):
        block = arrays[a].at[zmod(z + off), core]
        cp = remote(block, block, sib_s.at[a, i], sib_r.at[a, i], sibling)
        cp.start()
        started.append(cp)
        sibs.append(cp)

    def length(d, ch):
        return min(REACH, counts[d]) if ch == 0 else max(counts[d] - REACH, 0)

    flying = {}
    for a in range(2):
        for ch in (1, 0):
            for d in dirs:
                if length(d, ch) > 0:
                    flying[a, d, ch] = ring_send(a, d, ch, 0)
    row_bcast(ssq.at[row], ssq, ssq_s, ssq_r)
    for a in range(2):
        sib_send(a, 0, 0)
    kvt_cp = []
    for i, dev in enumerate((sibling, {"col": pair * 2 + core}, {"col": pair * 2 + 1 - core})):
        cp = remote(kvt.at[member], kvt.at[member], kvt_s.at[i], kvt_r.at[i], dev)
        cp.start()
        kvt_cp.append(cp)

    count = {0: 1, 1: 1}

    def ring_step(t):
        for a in range(2):
            for ch in (0, 1):
                for d in dirs:
                    if t >= length(d, ch):
                        continue
                    flying[a, d, ch].wait_recv()
                    if t + 1 < length(d, ch):
                        flying[a, d, ch] = ring_send(a, d, ch, t + 1)
                    sib_send(a, count[a], -d * (t + 1 + (REACH if ch else 0)))
                    count[a] += 1

    ring_step(0)
    each(R, lambda k: row_recv(ssq, ssq_r, ssq_s, k))
    total = ssq[0]
    for i in range(1, R):
        total = total + ssq[i]
    inv_own = lax.rsqrt(total * (1.0 / MODEL_WIDTH) + EPS)
    lane = lax.broadcasted_iota(jnp.int32, (B, 128), 1)
    hi = inv_own.astype(BF16).astype(F32)
    mid = (inv_own - hi).astype(BF16).astype(F32)
    lo = inv_own - hi - mid
    aux_all[z, core] = jnp.where(
        lane == 0, hi, jnp.where(lane == 1, mid, jnp.where(lane == 2, lo, aux0))
    ).astype(BF16)

    def aux_copy(k):
        return remote(aux_all.at[z, core], aux_all.at[z, core], aux_s.at[k], aux_r.at[z],
                      at_z(z + k))

    each(Z, lambda k: aux_copy(k).start())
    for t in range(1, REACH):
        ring_step(t)

    def aux_recv(k):
        s = zmod(z + k)
        remote(aux_all.at[s, core], aux_all.at[s, core], aux_s.at[k], aux_r.at[s],
               at_z(z + k)).wait_recv()

    each(Z, aux_recv)
    aux_half = remote(aux_all.at[:, core], aux_all.at[:, core], auxsib.at[0], auxsib.at[1], sibling)
    aux_half.start()
    for cp in sibs:
        cp.wait_recv()
    for cp in kvt_cp:
        cp.wait_recv()
    aux_half.wait_recv()

    kv_rows = jnp.concatenate(
        [kvt[g, half * 32:half * 32 + 32, :] for half in range(2) for g in range(GROUP)], axis=0)
    KV0 = 2 * H
    LOW0 = KV0 + 2 * HEAD
    chunks = Z // CH
    rows_c = CH * S

    def rs_copy(p):
        return remote(part.at[p], rx.at[row], rs_s.at[p], rs_r.at[row], {"row": p})

    def project(i, carry):
        q = lax.rem(lax.div(row, CH) + i, chunks)
        first = q * CH
        w = w_all[pl.ds(first, CH)].reshape(rows_c, D)
        h = h_all[pl.ds(first, CH)].reshape(rows_c, D).astype(F32)
        ax = aux_all[pl.ds(first, CH)].reshape(rows_c, 128).astype(F32)
        inv = ax[:, 0:1] + ax[:, 1:2] + ax[:, 2:3]
        n = (h * inv * gf).astype(BF16)
        n_all[pl.ds(first, CH)] = n.reshape(CH, S, D)
        span = pl.ds(first, CH)
        part[span, :, 0:H] = nt(w, wo[...]).astype(BF16).reshape(CH, S, H)
        part[span, :, H:KV0] = nn(n, wq[...]).astype(BF16).reshape(CH, S, H)
        part[span, :, KV0:LOW0] = nt(n, kv_rows).astype(BF16).reshape(CH, S, 2 * HEAD)
        part[span, :, LOW0:LOW0 + 128] = jnp.concatenate(
            [nt(w, oup[...]), nn(n, qdown[...])], axis=1).astype(BF16).reshape(CH, S, 128)
        for m in range(CH):
            p = first + lax.rem(row + m, CH)

            @pl.when(p != row)
            def _():
                rs_copy(p).start()
        return carry

    lax.fori_loop(0, chunks, project, 0)

    ax = aux_all[row].reshape(S, 128).astype(F32)
    pos = ax[:, 3:4] * 64.0 + ax[:, 4:5]
    lane_s = lax.broadcasted_iota(jnp.int32, (S, HEAD), 1)
    half_lane = lax.rem(lane_s, HEAD // 2).astype(F32)
    angle = pos * jnp.exp(half_lane * (-2.0 * math.log(BASE) / HEAD))
    cosine = jnp.cos(angle)
    sine = jnp.where(lane_s < HEAD // 2, -1.0, 1.0) * jnp.sin(angle)

    def swap(x):
        return jnp.concatenate([x[:, HEAD // 2:], x[:, :HEAD // 2]], axis=1)

    def rotate(x):
        return x * cosine + swap(x) * sine

    def unrotate(x):
        return x * cosine - swap(x) * sine

    pick = (lax.broadcasted_iota(jnp.int32, (8, 128), 1) == 5).astype(BF16)
    seg_key = nt(pick, aux_all[...].reshape(T, 128))[0:1, :]
    token = row * S + lax.broadcasted_iota(jnp.int32, (S, T), 0)
    allowed = (ax[:, 5:6] == seg_key) & (lax.broadcasted_iota(jnp.int32, (S, T), 1) <= token)
    allowed = jnp.concatenate([allowed.astype(F32)] * heads, axis=0) > 0.5

    acc = part[row].astype(F32)
    for k in range(1, R):
        row_recv(rx, rs_r, rs_s, k)
        acc = acc + rx[peer(k)].astype(F32)
    low = acc[:, LOW0:LOW0 + 128].astype(BF16)
    kvx[row, :, 0:HEAD] = rotate(acc[:, KV0:KV0 + HEAD]).astype(BF16)
    kvx[row, :, HEAD:2 * HEAD] = acc[:, KV0 + HEAD:LOW0].astype(BF16)
    kvx[row, :, 2 * HEAD:3 * HEAD] = low
    row_bcast(kvx.at[row], kvx, kvx_s, kvx_r)
    dA = (acc[:, 0:H] + 2.0 * nt(low[:, 0:RANK], odown[...])).astype(BF16)
    ql = acc[:, H:KV0] + 2.0 * nn(low[:, RANK:2 * RANK], qup[...])
    queries = jnp.concatenate(
        [rotate(ql[:, i * HEAD:(i + 1) * HEAD]).astype(BF16) for i in range(heads)], axis=0)
    grads = jnp.concatenate([dA[:, i * HEAD:(i + 1) * HEAD] for i in range(heads)], axis=0)
    each(R, lambda k: row_recv(kvx, kvx_r, kvx_s, k))

    keys = kvx[:, :, 0:HEAD].reshape(T, HEAD)
    values = kvx[:, :, HEAD:2 * HEAD].reshape(T, HEAD)
    scores = jnp.where(allowed, nt(queries, keys) * SCALE, FILL)
    shifted = jnp.exp(scores - jnp.max(scores, axis=1, keepdims=True))
    probs = shifted / jnp.sum(shifted, axis=1, keepdims=True)
    narrow = probs.astype(BF16)
    pgrad = nt(grads, values)
    rdot = jnp.sum(probs * pgrad, axis=1, keepdims=True)
    sgrad = (probs * (pgrad - rdot) * SCALE).astype(BF16)
    kvpart[:, :, 0:HEAD] = tn(sgrad, queries).astype(BF16).reshape(R, S, HEAD)
    kvpart[:, :, HEAD:2 * HEAD] = tn(narrow, grads).astype(BF16).reshape(R, S, HEAD)

    def kvp_copy(k):
        return remote(kvpart.at[peer(k)], kvrx.at[row], kvp_s.at[k], kvp_r.at[row],
                      {"row": peer(k)})

    each(R, lambda k: kvp_copy(k).start())
    qg = nn(sgrad, keys)
    for i in range(heads):
        qg_all[row, :, i * HEAD:(i + 1) * HEAD] = unrotate(qg[i * S:(i + 1) * S]).astype(BF16)
    row_bcast(qg_all.at[row], qg_all, qg_s, qg_r)
    att = nn(narrow, values).astype(BF16)
    for i in range(heads):
        att_all[row, :, i * HEAD:(i + 1) * HEAD] = att[i * S:(i + 1) * S]
    kacc = kvpart[row].astype(F32)
    for k in range(1, R):
        row_recv(kvrx, kvp_r, kvp_s, k)
        kacc = kacc + kvrx[peer(k)].astype(F32)
    kvg_all[row, :, 0:HEAD] = unrotate(kacc[:, 0:HEAD]).astype(BF16)
    kvg_all[row, :, HEAD:2 * HEAD] = kacc[:, HEAD:2 * HEAD].astype(BF16)
    row_bcast(kvg_all.at[row], kvg_all, kvg_s, kvg_r)
    row_bcast(att_all.at[row], att_all, att_s, att_r)
    each(R, lambda k: row_recv(qg_all, qg_r, qg_s, k))
    each(R, lambda k: row_recv(kvg_all, kvg_r, kvg_s, k))
    each(R, lambda k: row_recv(att_all, att_r, att_s, k))

    def sg_copy(q):
        span = pl.ds(q * CH, CH)
        return remote(sib_out.at[span], sib_in.at[span], sg_s.at[q], sg_r.at[q], sibling)

    def backward(i, carry):
        q = lax.rem(lax.div(z, CH) + chunks // 2 + i, chunks)
        span = pl.ds(q * CH, CH)
        qrows = qg_all[span].reshape(rows_c, H)
        krows = kvg_all[span].reshape(rows_c, 2 * HEAD)
        arows = att_all[span].reshape(rows_c, H)
        g = nt(qrows, wq[...]) + nn(krows, kv_rows)
        lows = jnp.concatenate([nn(arows, odown[...]), nt(qrows, qup[...])], axis=1)
        g = g.reshape(CH, 2, B, D)
        lows = lows.reshape(CH, 2, B, 128)
        mine = core == 0
        own[span, :, 0:D] = jnp.where(mine, g[:, 0], g[:, 1])
        own[span, :, D:D + 128] = jnp.where(mine, lows[:, 0], lows[:, 1])
        sib_out[span, :, 0:D] = jnp.where(mine, g[:, 1], g[:, 0]).astype(BF16)
        sib_out[span, :, D:D + 128] = jnp.where(mine, lows[:, 1], lows[:, 0]).astype(BF16)
        sg_copy(q).start()
        return carry

    lax.fori_loop(0, chunks, backward, 0)

    def add_sibling(i, carry):
        q = lax.rem(lax.div(z, CH) + chunks // 2 + i, chunks)
        span = pl.ds(q * CH, CH)
        sg_copy(q).wait_recv()
        own[span] = own[span] + sib_in[span].astype(F32)
        return carry

    lax.fori_loop(0, chunks, add_sibling, 0)

    hops = {}

    def hop(d, ch, t):
        i = 0 if d == 1 else 1
        far = ch == 1 and t == REACH - 1
        return remote(hop_out.at[i, ch, t], hop_in.at[i, ch, t], hop_s.at[i, ch, t],
                      hop_r.at[i, ch, t], at_z(z + d * (REACH + 1 if far else 1)))

    for t in range(REACH):
        for ch in (1, 0):
            for d in dirs:
                delta = REACH - t + (REACH if ch else 0)
                last = REACH if ch == 0 else counts[d]
                if delta > last:
                    continue
                i = 0 if d == 1 else 1
                term = own[zmod(z + d * delta)]
                if delta < last:
                    hops[d, ch, t - 1].wait_recv()
                    term = term + hop_in[i, ch, t - 1].astype(F32)
                hop_out[i, ch, t] = term.astype(BF16)
                hops[d, ch, t] = hop(d, ch, t)
                hops[d, ch, t].start()

    lows_all = kvx[:, :, 2 * HEAD:3 * HEAD].reshape(T, 128)
    qup_g[...] = 2.0 * tn(lows_all, qg_all[...].reshape(T, H))[RANK:2 * RANK]
    odown_g[...] = 2.0 * tn(att_all[...].reshape(T, H), lows_all[:, 0:RANK])

    final = own[z]
    for ch in (0, 1):
        for d in dirs:
            if length(d, ch) > 0:
                hops[d, ch, REACH - 1].wait_recv()
                final = final + hop_in[0 if d == 1 else 1, ch, REACH - 1].astype(F32)

    low_all[z, core] = final[:, D:D + 128].astype(BF16)

    def low_copy(k):
        return remote(low_all.at[z, core], low_all.at[z, core], low_s.at[k], low_r.at[z],
                      at_z(z + k))

    each(Z, lambda k: low_copy(k).start())
    low_back = final[:, D + RANK:D + 2 * RANK].astype(BF16)
    ngrad = final[:, 0:D] + 2.0 * nt(low_back, qdown[...])
    dots[row] = jnp.broadcast_to(
        jnp.sum(hf * gf * ngrad, axis=1, keepdims=True), (B, 128))
    row_bcast(dots.at[row], dots, dot_s, dot_r)

    def low_recv(k):
        s = zmod(z + k)
        remote(low_all.at[s, core], low_all.at[s, core], low_s.at[k], low_r.at[s],
               at_z(z + k)).wait_recv()

    each(Z, low_recv)
    low_half = remote(low_all.at[:, core], low_all.at[:, core], lowsib.at[0], lowsib.at[1], sibling)
    low_half.start()
    each(R, lambda k: row_recv(dots, dot_r, dot_s, k))
    dsum = dots[0]
    for i in range(1, R):
        dsum = dsum + dots[i]
    inv = inv_own[:, 0:1]
    igrad[...] = (
        w_own.astype(F32) + inv * gf * ngrad
        - hf * (inv * inv * inv * dsum[:, 0:1] * (1.0 / MODEL_WIDTH)))
    low_half.wait_recv()
    lb = low_all[...].reshape(T, 128)
    oup_g[...] = 2.0 * tn(lb, w_all[...].reshape(T, D))[0:RANK]
    qdown_g[...] = 2.0 * tn(n_all[...].reshape(T, D), lb)[:, RANK:2 * RANK]

    for cp in started:
        cp.wait_send()
    for cp in kvt_cp:
        cp.wait_send()
    row_done(ssq.at[row], ssq, ssq_s, ssq_r)
    each(Z, lambda k: aux_copy(k).wait_send())
    aux_half.wait_send()
    each(R, lambda k: rs_copy(peer(k)).wait_send())
    row_done(kvx.at[row], kvx, kvx_s, kvx_r)
    each(R, lambda k: kvp_copy(k).wait_send())
    row_done(qg_all.at[row], qg_all, qg_s, qg_r)
    row_done(kvg_all.at[row], kvg_all, kvg_s, kvg_r)
    row_done(att_all.at[row], att_all, att_s, att_r)
    for q in range(chunks):
        sg_copy(q).wait_send()
    for cp in hops.values():
        cp.wait_send()
    each(Z, lambda k: low_copy(k).wait_send())
    low_half.wait_send()
    row_done(dots.at[row], dots, dot_s, dot_r)


def per_device(
    hidden, cotangent, importance, positions, segments, norm_gain, query_weight_matrix,
    key_weight, value_weight_matrix, output_weight_matrix, query_down_factor, query_up_factor,
    output_down_factor, out_up,
):
    R = lax.axis_size("row")
    C = lax.axis_size("col")
    Z = C // 2
    B, D = hidden.shape
    H = query_weight_matrix.shape[1]
    S = 2 * B
    T = B * C
    W = 2 * H + 2 * HEAD + 128
    lane = jnp.arange(128)[None, :]
    cols = (
        (3, (positions // 64).astype(F32)),
        (4, (positions % 64).astype(F32)),
        (5, segments.astype(F32)),
        (6, jnp.minimum(importance.astype(F32), CAP)),
    )
    aux = jnp.zeros((B, 128), F32)
    for i, v in cols:
        aux = jnp.where(lane == i, v[:, None], aux)
    kvt = jnp.concatenate([key_weight, value_weight_matrix], axis=1).T
    vmem = pl.BlockSpec(memory_space=pltpu.VMEM)
    dma = pltpu.SemaphoreType.DMA
    outs = (
        jax.ShapeDtypeStruct((B, D), F32),
        jax.ShapeDtypeStruct((D, RANK), F32),
        jax.ShapeDtypeStruct((RANK, H), F32),
        jax.ShapeDtypeStruct((H, RANK), F32),
        jax.ShapeDtypeStruct((RANK, D), F32),
    )
    scratch = [
        pltpu.VMEM((Z, 2, B, D), BF16),
        pltpu.VMEM((Z, 2, B, D), BF16),
        pltpu.VMEM((Z, S, D), BF16),
        pltpu.VMEM((Z, 2, B, 128), BF16),
        pltpu.VMEM((GROUP, 64, D), BF16),
        pltpu.VMEM((R, B, 128), F32),
        pltpu.VMEM((R, S, W), BF16),
        pltpu.VMEM((R, S, W), BF16),
        pltpu.VMEM((R, S, 3 * HEAD), BF16),
        pltpu.VMEM((R, S, 2 * HEAD), BF16),
        pltpu.VMEM((R, S, 2 * HEAD), BF16),
        pltpu.VMEM((R, S, H), BF16),
        pltpu.VMEM((R, S, 2 * HEAD), BF16),
        pltpu.VMEM((R, S, H), BF16),
        pltpu.VMEM((R, B, 128), F32),
        pltpu.VMEM((Z, B, D + 128), F32),
        pltpu.VMEM((Z, B, D + 128), BF16),
        pltpu.VMEM((Z, B, D + 128), BF16),
        pltpu.VMEM((2, 2, REACH, B, D + 128), BF16),
        pltpu.VMEM((2, 2, REACH, B, D + 128), BF16),
        pltpu.VMEM((Z, 2, B, 128), BF16),
        dma((2, 2, 2, REACH)), dma((2, 2, 2, REACH)),
        dma((2, Z)), dma((2, Z)),
        dma((R,)), dma((R,)),
        dma((Z,)), dma((Z,)), dma((2,)),
        dma((3,)), dma((3,)),
        dma((R,)), dma((R,)),
        dma((R,)), dma((R,)),
        dma((R,)), dma((R,)),
        dma((R,)), dma((R,)),
        dma((R,)), dma((R,)),
        dma((R,)), dma((R,)),
        dma((Z,)), dma((Z,)),
        dma((2, 2, REACH)), dma((2, 2, REACH)),
        dma((Z,)), dma((Z,)), dma((2,)),
        dma((R,)), dma((R,)),
    ]
    return tuple(pl.pallas_call(
        functools.partial(kernel, R, Z),
        out_shape=outs,
        in_specs=[vmem] * 11,
        out_specs=[vmem] * 5,
        scratch_shapes=scratch,
        compiler_params=pltpu.CompilerParams(
            collective_id=0, has_side_effects=True, vmem_limit_bytes=56 * 1024 * 1024),
        name="attention_backward",
    )(
        hidden, cotangent, aux, norm_gain.reshape(1, D), query_weight_matrix,
        query_down_factor, kvt.reshape(2 * (H // 16), D), output_weight_matrix, out_up,
        output_down_factor, query_up_factor,
    ))


def solution(mesh):
    placed = (
        P("col", "row"), P("col", "row"), P("col"), P("col"), P("col"), P("row"),
        P("row", "col"), P("row", "col"), P("row", "col"), P("col", "row"),
        P("row", None), P(None, "col"), P("col", None), P(None, "row"),
    )
    return jax.shard_map(
        per_device,
        mesh=mesh,
        in_specs=placed,
        out_specs=(P("col", "row"), P("row", None), P(None, "col"), P("col", None), P(None, "row")),
        check_vma=False,
    )
```

```python
import functools
import math

import jax
import jax.numpy as jnp
from jax import lax
from jax.experimental import pallas as pl
from jax.experimental.pallas import tpu as pltpu
from jax.sharding import PartitionSpec as P

MODEL_WIDTH = 16384
HEAD = 128
RANK = 64
GROUP = 4
EPS = 1e-05
CAP = 2.0
BASE = 500000.0
FILL = -1e30
SCALE = HEAD**-0.5
MESH = pl.DeviceIdType.MESH
F32 = jnp.float32
BF16 = jnp.bfloat16
REACH = 4


def nn(a, b):
    return lax.dot_general(a, b, (((1,), (0,)), ((), ())), preferred_element_type=F32)


def nt(a, b):
    return lax.dot_general(a, b, (((1,), (1,)), ((), ())), preferred_element_type=F32)


def tn(a, b):
    return lax.dot_general(a, b, (((0,), (0,)), ((), ())), preferred_element_type=F32)


def remote(src, dst, send, recv, device):
    return pltpu.make_async_remote_copy(
        src_ref=src, dst_ref=dst, send_sem=send, recv_sem=recv,
        device_id=device, device_id_type=MESH,
    )


def kernel(
    R, Z,
    hid, cot, imp, posn, segm, gain, wq, qdown_t, kw_t, vw_t, wo, oup, odown_t, qup,
    igrad, qdown_g, qup_g, odown_g, oup_g,
    h_all, w_all, n_all, aux_all, kvt,
    ssq, part_w, rx_w, part_kv, rx_kv, part_q, rx_q, kvx, lowx, kvpart, kvrx,
    qg_all, kvg_all, att_all, dots,
    lown, lowz, low_all, gq, own, sib_out, sib_in, hop_out, hop_in,
    ring_s, ring_r, sib_s, sib_r, ssq_s, ssq_r, aux_s, aux_r, auxsib, kvt_s, kvt_r,
    rsw_s, rsw_r, rsk_s, rsk_r, rsq_s, rsq_r, kvx_s, kvx_r, lowx_s, lowx_r,
    kvp_s, kvp_r, qg_s, qg_r, kvg_s, kvg_r, att_s, att_r,
    lowp, lowz_s, lowz_r, low_s, low_r, lowsib, sg_s, sg_r, hop_s, hop_r, dot_s, dot_r,
):
    row = lax.axis_index("row")
    col = lax.axis_index("col")
    z = lax.div(col, 2)
    core = lax.rem(col, 2)
    B, D = hid.shape
    S = 2 * B
    T = S * Z
    H = wo.shape[0]
    heads = H // HEAD
    counts = {1: Z // 2, -1: Z - 1 - Z // 2}
    dirs = (1, -1)
    drains = []

    def zmod(v):
        return lax.rem(v + 2 * Z, Z)

    def at_z(v):
        return {"col": zmod(v) * 2 + core}

    sibling = {"col": z * 2 + 1 - core}
    pair = z + 1 - 2 * lax.rem(z, 2)

    def peer(k):
        return lax.rem(row + k, R)

    def each(n, f):
        def step(k, carry):
            f(k)
            return carry
        lax.fori_loop(1, n, step, 0)

    def start(cp):
        cp.start()
        drains.append(cp.wait_send)
        return cp

    def row_copy(src, dst, ss, rs, k):
        return remote(src, dst, ss.at[k], rs, {"row": peer(k)})

    def row_bcast(src, dst_all, ss, rs):
        def one(k):
            return row_copy(src, dst_all.at[row], ss, rs.at[row], k)
        each(R, lambda k: one(k).start())
        drains.append(lambda: each(R, lambda k: one(k).wait_send()))

    def row_recv(dst_all, rs, ss, k):
        s = peer(k)
        row_copy(dst_all.at[s], dst_all.at[s], ss, rs.at[s], k).wait_recv()

    def z_bcast(src, dst_of, ss, rs):
        def one(k):
            return remote(src, dst_of(z), ss.at[k], rs.at[z], at_z(z + k))
        each(Z, lambda k: one(k).start())
        drains.append(lambda: each(Z, lambda k: one(k).wait_send()))

    def z_recv(dst_of, ss, rs):
        def one(k):
            s = zmod(z + k)
            remote(dst_of(s), dst_of(s), ss.at[k], rs.at[s], at_z(z + k)).wait_recv()
        each(Z, one)

    barrier = pltpu.get_barrier_semaphore()
    each(R, lambda k: pl.semaphore_signal(
        barrier, inc=1, device_id={"row": peer(k)}, device_id_type=MESH))
    each(Z, lambda k: pl.semaphore_signal(
        barrier, inc=1, device_id=at_z(z + k), device_id_type=MESH))
    pl.semaphore_signal(barrier, inc=1, device_id=sibling, device_id_type=MESH)
    pl.semaphore_signal(
        barrier, inc=1, device_id={"col": pair * 2 + 1 - core}, device_id_type=MESH)

    diagonal = (lax.broadcasted_iota(jnp.int32, (B, B), 0)
                == lax.broadcasted_iota(jnp.int32, (B, B), 1))

    def column(v):
        return jnp.sum(jnp.where(diagonal, v.reshape(1, B), 0.0), axis=1, keepdims=True)

    hf = hid[...].astype(F32)
    gf = gain[...].astype(F32).reshape(1, D)
    w_own = (cot[...].astype(F32)
             * column(jnp.minimum(imp[...].astype(F32), CAP))).astype(BF16)
    w_all[z, core] = w_own
    h_all[z, core] = hid[...]
    ssq[row] = jnp.broadcast_to(jnp.sum(hf * hf, axis=1, keepdims=True), (B, 128))
    member = lax.rem(col, GROUP)
    kvt[0, member] = kw_t[...]
    kvt[1, member] = vw_t[...]
    pl.semaphore_wait(barrier, R - 1 + Z - 1 + 2)

    arrays = (w_all, h_all)

    def length(d, ch):
        return min(REACH, counts[d]) if ch == 0 else max(counts[d] - REACH, 0)

    def ring_send(a, d, ch, t):
        off = t if ch == 0 else (0 if t == 0 else REACH + t)
        block = arrays[a].at[zmod(z - d * off), core]
        target = z + d * (REACH + 1 if ch == 1 and t == 0 else 1)
        i = 0 if d == 1 else 1
        return start(remote(
            block, block, ring_s.at[a, i, ch, t], ring_r.at[a, i, ch, t], at_z(target)))

    halves = {}

    def sib_send(a, t, i, off):
        block = arrays[a].at[zmod(z + off), core]
        cp = start(remote(block, block, sib_s.at[a, t, i], sib_r.at[a, t, i], sibling))
        halves.setdefault((a, t), []).append(cp)

    flying = {}
    for a in range(2):
        for ch in (1, 0):
            for d in dirs:
                if length(d, ch) > 0:
                    flying[a, d, ch] = ring_send(a, d, ch, 0)
    row_bcast(ssq.at[row], ssq, ssq_s, ssq_r)
    for a in range(2):
        sib_send(a, REACH - 1, 3, 0)

    def ring_step(t):
        for a in range(2):
            i = 0
            for ch in (1, 0):
                for d in dirs:
                    if t >= length(d, ch):
                        continue
                    flying[a, d, ch].wait_recv()
                    if t + 1 < length(d, ch):
                        flying[a, d, ch] = ring_send(a, d, ch, t + 1)
                    sib_send(a, t, i, -d * (t + 1 + (REACH if ch else 0)))
                    i += 1

    def chips_of(t):
        found = [-d * (t + 1 + (REACH if ch else 0))
                 for ch in (1, 0) for d in dirs if t < length(d, ch)]
        return found + [0] if t == REACH - 1 else found

    groups = [chips_of(t) for t in range(REACH)]

    kvt_cp = []
    for i, dev in enumerate((sibling, {"col": pair * 2 + core}, {"col": pair * 2 + 1 - core})):
        for half in range(2):
            kvt_cp.append(start(remote(
                kvt.at[half, member], kvt.at[half, member], kvt_s.at[i, half],
                kvt_r.at[i, half], dev)))
    ring_step(0)
    each(R, lambda k: row_recv(ssq, ssq_r, ssq_s, k))
    total = ssq[0]
    for i in range(1, R):
        total = total + ssq[i]
    inv_own = lax.rsqrt(total * (1.0 / MODEL_WIDTH) + EPS)
    lane = lax.broadcasted_iota(jnp.int32, (B, 128), 1)
    hi = inv_own.astype(BF16).astype(F32)
    mid = (inv_own - hi).astype(BF16).astype(F32)
    lo = inv_own - hi - mid
    p_own = posn[...]
    p_hi = lax.div(p_own, 64)
    tile = jnp.where(lane == 0, hi, jnp.where(lane == 1, mid, lo))
    for i, v in ((3, p_hi), (4, p_own - p_hi * 64), (5, segm[...])):
        tile = jnp.where(lane == i, column(v.astype(F32)), tile)
    aux_all[z, core] = tile.astype(BF16)
    z_bcast(aux_all.at[z, core], lambda s: aux_all.at[s, core], aux_s, aux_r)

    def rs_copy(src, dst, ss, rs, p):
        return remote(src.at[p], dst.at[row], ss.at[p], rs.at[row], {"row": p})

    def rs_send(group, src, dst, ss, rs):
        n = len(group)
        for m in range(n):
            turn = lax.rem(row + m, n)
            delta = group[0]
            for i in range(1, n):
                delta = jnp.where(turn == i, group[i], delta)
            p = zmod(z + delta)

            @pl.when(p != row)
            def _():
                rs_copy(src, dst, ss, rs, p).start()

    def rs_drain(src, dst, ss, rs):
        drains.append(lambda: each(R, lambda k: rs_copy(src, dst, ss, rs, peer(k)).wait_send()))

    def rows_of(ref, group, width):
        return jnp.concatenate(
            [ref[zmod(z + o)].reshape(S, width) for o in group], axis=0)

    def store(ref, group, value, at=slice(None)):
        for i, o in enumerate(group):
            ref[zmod(z + o), :, at] = value[i * S:(i + 1) * S]

    def project_w(t):
        g = groups[t]
        for cp in halves[0, t]:
            cp.wait_recv()
        store(part_w, g, nt(rows_of(w_all, g, D), wo[...]).astype(BF16))
        rs_send(g, part_w, rx_w, rsw_s, rsw_r)

    def project_kv(t):
        g = groups[t]
        for cp in halves[1, t]:
            cp.wait_recv()
        ax = rows_of(aux_all, g, 128).astype(F32)
        h = rows_of(h_all, g, D).astype(F32)
        n = (h * (ax[:, 0:1] + ax[:, 1:2] + ax[:, 2:3]) * gf).astype(BF16)
        store(n_all, g, n)
        store(part_kv, g, nt(n, kvt[...].reshape(2 * HEAD, D)).astype(BF16), slice(0, 2 * HEAD))
        store(part_kv, g, jnp.concatenate(
            [nt(rows_of(w_all, g, D), oup[...]), nt(n, qdown_t[...])], axis=1).astype(BF16),
            slice(2 * HEAD, 3 * HEAD))
        rs_send(g, part_kv, rx_kv, rsk_s, rsk_r)

    def project_q(t):
        g = groups[t]
        store(part_q, g, nn(rows_of(n_all, g, D), wq[...]).astype(BF16))
        rs_send(g, part_q, rx_q, rsq_s, rsq_r)

    ring_step(1)
    project_w(0)
    ring_step(2)
    project_w(1)
    z_recv(lambda s: aux_all.at[s, core], aux_s, aux_r)
    aux_half = start(remote(
        aux_all.at[:, core], aux_all.at[:, core], auxsib.at[0], auxsib.at[1], sibling))
    ring_step(3)
    project_w(2)
    aux_half.wait_recv()
    for cp in kvt_cp:
        cp.wait_recv()
    for t in range(3):
        project_kv(t)
    project_w(3)
    project_kv(3)
    for t in range(4):
        project_q(t)
    rs_drain(part_w, rx_w, rsw_s, rsw_r)
    rs_drain(part_kv, rx_kv, rsk_s, rsk_r)
    rs_drain(part_q, rx_q, rsq_s, rsq_r)

    ax = aux_all[row].reshape(S, 128).astype(F32)
    pos = ax[:, 3:4] * 64.0 + ax[:, 4:5]
    lane_s = lax.broadcasted_iota(jnp.int32, (S, HEAD), 1)
    half_lane = lax.rem(lane_s, HEAD // 2).astype(F32)
    angle = pos * jnp.exp(half_lane * (-2.0 * math.log(BASE) / HEAD))
    cosine = jnp.cos(angle)
    sine = jnp.where(lane_s < HEAD // 2, -1.0, 1.0) * jnp.sin(angle)

    def swap(x):
        return jnp.concatenate([x[:, HEAD // 2:], x[:, :HEAD // 2]], axis=1)

    def rotate(x):
        return x * cosine + swap(x) * sine

    def unrotate(x):
        return x * cosine - swap(x) * sine

    pick = (lax.broadcasted_iota(jnp.int32, (8, 128), 1) == 5).astype(BF16)
    seg_key = nt(pick, aux_all[...].reshape(T, 128))[0:1, :]
    token = row * S + lax.broadcasted_iota(jnp.int32, (S, T), 0)
    allowed = (ax[:, 5:6] == seg_key) & (lax.broadcasted_iota(jnp.int32, (S, T), 1) <= token)
    allowed = jnp.concatenate([allowed.astype(F32)] * heads, axis=0) > 0.5

    def rs_sum(part, rx, ss, rs):
        acc = part[row].astype(F32)
        for k in range(1, R):
            row_recv(rx, rs, ss, k)
            acc = acc + rx[peer(k)].astype(F32)
        return acc

    dA = rs_sum(part_w, rx_w, rsw_s, rsw_r)
    kvl = rs_sum(part_kv, rx_kv, rsk_s, rsk_r)
    kvx[row, :, 0:HEAD] = rotate(kvl[:, 0:HEAD]).astype(BF16)
    kvx[row, :, HEAD:2 * HEAD] = kvl[:, HEAD:2 * HEAD].astype(BF16)
    row_bcast(kvx.at[row], kvx, kvx_s, kvx_r)
    low = kvl[:, 2 * HEAD:3 * HEAD].astype(BF16)
    lowx[row] = low
    row_bcast(lowx.at[row], lowx, lowx_s, lowx_r)
    dA = (dA + 2.0 * nn(low[:, 0:RANK], odown_t[...])).astype(BF16)
    grads = jnp.concatenate([dA[:, i * HEAD:(i + 1) * HEAD] for i in range(heads)], axis=0)
    ql = 2.0 * nn(low[:, RANK:2 * RANK], qup[...])
    ql = ql + rs_sum(part_q, rx_q, rsq_s, rsq_r)
    queries = jnp.concatenate(
        [rotate(ql[:, i * HEAD:(i + 1) * HEAD]).astype(BF16) for i in range(heads)], axis=0)
    each(R, lambda k: row_recv(kvx, kvx_r, kvx_s, k))

    keys = kvx[:, :, 0:HEAD].reshape(T, HEAD)
    values = kvx[:, :, HEAD:2 * HEAD].reshape(T, HEAD)
    scores = jnp.where(allowed, nt(queries, keys) * SCALE, FILL)
    shifted = jnp.exp(scores - jnp.max(scores, axis=1, keepdims=True))
    probs = shifted / jnp.sum(shifted, axis=1, keepdims=True)
    narrow = probs.astype(BF16)
    pgrad = nt(grads, values)
    rdot = jnp.sum(probs * pgrad, axis=1, keepdims=True)
    sgrad = (probs * (pgrad - rdot) * SCALE).astype(BF16)
    kvpart[:, :, 0:HEAD] = tn(sgrad, queries).astype(BF16).reshape(R, S, HEAD)
    kvpart[:, :, HEAD:2 * HEAD] = tn(narrow, grads).astype(BF16).reshape(R, S, HEAD)

    def kvp_copy(k):
        return remote(kvpart.at[peer(k)], kvrx.at[row], kvp_s.at[k], kvp_r.at[row],
                      {"row": peer(k)})

    each(R, lambda k: kvp_copy(k).start())
    drains.append(lambda: each(R, lambda k: kvp_copy(k).wait_send()))
    qg = nn(sgrad, keys)
    for i in range(heads):
        qg_all[row, :, i * HEAD:(i + 1) * HEAD] = unrotate(qg[i * S:(i + 1) * S]).astype(BF16)
    row_bcast(qg_all.at[row], qg_all, qg_s, qg_r)
    att = nn(narrow, values).astype(BF16)
    for i in range(heads):
        att_all[row, :, i * HEAD:(i + 1) * HEAD] = att[i * S:(i + 1) * S]

    inner = jnp.concatenate(
        [nt(att_all[row], odown_t[...]), nt(qg_all[row], qup[...])], axis=1)
    lown[0] = jnp.where(core == 0, inner[0:B], inner[B:S])
    lown[1] = jnp.where(core == 0, inner[B:S], inner[0:B])
    low_pair = start(remote(lown.at[1], lown.at[2], lowp.at[0], lowp.at[1], sibling))
    kacc = rs_sum(kvpart, kvrx, kvp_s, kvp_r)
    kvg_all[row, :, 0:HEAD] = unrotate(kacc[:, 0:HEAD]).astype(BF16)
    kvg_all[row, :, HEAD:2 * HEAD] = kacc[:, HEAD:2 * HEAD].astype(BF16)
    row_bcast(kvg_all.at[row], kvg_all, kvg_s, kvg_r)
    low_pair.wait_recv()
    lowz[z] = lown[0] + lown[2]
    z_bcast(lowz.at[z], lambda s: lowz.at[s], lowz_s, lowz_r)
    row_bcast(att_all.at[row], att_all, att_s, att_r)

    each(R, lambda k: row_recv(qg_all, qg_r, qg_s, k))
    order = list(reversed(range(REACH)))
    for t in order:
        gq[t, 0:len(groups[t]) * S] = nt(rows_of(qg_all, groups[t], H), wq[...])
    z_recv(lambda s: lowz.at[s], lowz_s, lowz_r)
    inner = lowz[0]
    for i in range(1, Z):
        inner = inner + lowz[i]
    low_all[row, core] = inner.astype(BF16)
    row_bcast(low_all.at[row, core], low_all.at[:, core], low_s, low_r)
    each(R, lambda k: row_recv(kvg_all, kvg_r, kvg_s, k))

    def backward(t):
        g = groups[t]
        value = gq[t, 0:len(g) * S] + nn(
            rows_of(kvg_all, g, 2 * HEAD), kvt[...].reshape(2 * HEAD, D))
        value = value.reshape(len(g), 2, B, D)
        mine = core == 0
        sib_out[t, 0:len(g)] = jnp.where(mine, value[:, 1], value[:, 0]).astype(BF16)
        cp = start(remote(sib_out.at[t, pl.ds(0, len(g))], sib_in.at[t, pl.ds(0, len(g))],
                          sg_s.at[t], sg_r.at[t], sibling))
        own[t, 0:len(g)] = jnp.where(mine, value[:, 0], value[:, 1])
        return cp

    hops = {}

    def hop(d, ch, t):
        i = 0 if d == 1 else 1
        far = ch == 1 and t == REACH - 1
        return remote(hop_out.at[i, ch, t], hop_in.at[i, ch, t], hop_s.at[i, ch, t],
                      hop_r.at[i, ch, t], at_z(z + d * (REACH + 1 if far else 1)))

    def hop_step(t, cp):
        u = REACH - 1 - t
        cp.wait_recv()
        for ch in (1, 0):
            for d in dirs:
                delta = u + 1 + (REACH if ch else 0)
                last = REACH if ch == 0 else counts[d]
                if delta > last:
                    continue
                i = 0 if d == 1 else 1
                slot = groups[u].index(d * delta if d * delta in groups[u] else -d * delta)
                term = own[u, slot] + sib_in[u, slot].astype(F32)
                if delta < last:
                    hops[d, ch, t - 1].wait_recv()
                    term = term + hop_in[i, ch, t - 1].astype(F32)
                hop_out[i, ch, t] = term.astype(BF16)
                hops[d, ch, t] = start(hop(d, ch, t))

    sibs = {}
    for t, u in enumerate(order):
        sibs[t] = backward(u)
        if t > 0:
            hop_step(t - 1, sibs[t - 1])
    own_slot = groups[REACH - 1].index(0)
    final = own[REACH - 1, own_slot] + sib_in[REACH - 1, own_slot].astype(F32)
    low_all_row = low_all.at[:, core]
    each(R, lambda k: row_recv(low_all_row, low_r, low_s, k))
    low_half = start(remote(low_all_row, low_all_row, lowsib.at[0], lowsib.at[1], sibling))
    hop_step(REACH - 1, sibs[REACH - 1])
    each(R, lambda k: row_recv(lowx, lowx_r, lowx_s, k))
    lows_all = lowx[...].reshape(T, 128)
    qup_g[...] = 2.0 * tn(lows_all, qg_all[...].reshape(T, H))[RANK:2 * RANK]
    low_half.wait_recv()
    lb = low_all[...].reshape(T, 128)
    oup_g[...] = 2.0 * tn(lb, w_all[...].reshape(T, D))[0:RANK]
    qdown_g[...] = 2.0 * tn(lb, n_all[...].reshape(T, D))[RANK:2 * RANK]
    low_back = low_all[z, core][:, RANK:2 * RANK]
    final = final + 2.0 * nn(low_back, qdown_t[...])
    for ch in (0, 1):
        for d in dirs:
            if length(d, ch) > 0:
                hops[d, ch, REACH - 1].wait_recv()
                final = final + hop_in[0 if d == 1 else 1, ch, REACH - 1].astype(F32)
    dots[row] = jnp.broadcast_to(
        jnp.sum(hf * gf * final, axis=1, keepdims=True), (B, 128))
    row_bcast(dots.at[row], dots, dot_s, dot_r)
    each(R, lambda k: row_recv(att_all, att_r, att_s, k))
    odown_g[...] = 2.0 * tn(lows_all, att_all[...].reshape(T, H))[0:RANK]
    inv = inv_own[:, 0:1]
    base = w_own.astype(F32) + inv * gf * final
    each(R, lambda k: row_recv(dots, dot_r, dot_s, k))
    dsum = dots[0]
    for i in range(1, R):
        dsum = dsum + dots[i]
    igrad[...] = base - hf * (inv * inv * inv * dsum[:, 0:1] * (1.0 / MODEL_WIDTH))

    for wait in drains:
        wait()


def per_device(
    hidden, cotangent, importance, positions, segments, norm_gain, query_weight_matrix,
    key_weight, value_weight_matrix, output_weight_matrix, query_down_factor, query_up_factor,
    output_down_factor, out_up,
):
    R = lax.axis_size("row")
    C = lax.axis_size("col")
    Z = C // 2
    B, D = hidden.shape
    H = query_weight_matrix.shape[1]
    S = 2 * B
    CH = Z // REACH
    vmem = pl.BlockSpec(memory_space=pltpu.VMEM)
    dma = pltpu.SemaphoreType.DMA
    outs = (
        jax.ShapeDtypeStruct((B, D), F32),
        jax.ShapeDtypeStruct((RANK, D), F32),
        jax.ShapeDtypeStruct((RANK, H), F32),
        jax.ShapeDtypeStruct((RANK, H), F32),
        jax.ShapeDtypeStruct((RANK, D), F32),
    )
    scratch = [
        pltpu.VMEM((Z, 2, B, D), BF16),
        pltpu.VMEM((Z, 2, B, D), BF16),
        pltpu.VMEM((Z, S, D), BF16),
        pltpu.VMEM((Z, 2, B, 128), BF16),
        pltpu.VMEM((2, GROUP, HEAD // GROUP, D), BF16),
        pltpu.VMEM((R, B, 128), F32),
        pltpu.VMEM((R, S, H), BF16),
        pltpu.VMEM((R, S, H), BF16),
        pltpu.VMEM((R, S, 3 * HEAD), BF16),
        pltpu.VMEM((R, S, 3 * HEAD), BF16),
        pltpu.VMEM((R, S, H), BF16),
        pltpu.VMEM((R, S, H), BF16),
        pltpu.VMEM((R, S, 2 * HEAD), BF16),
        pltpu.VMEM((R, S, 128), BF16),
        pltpu.VMEM((R, S, 2 * HEAD), BF16),
        pltpu.VMEM((R, S, 2 * HEAD), BF16),
        pltpu.VMEM((R, S, H), BF16),
        pltpu.VMEM((R, S, 2 * HEAD), BF16),
        pltpu.VMEM((R, S, H), BF16),
        pltpu.VMEM((R, B, 128), F32),
        pltpu.VMEM((3, B, 128), F32),
        pltpu.VMEM((Z, B, 128), F32),
        pltpu.VMEM((R, 2, B, 128), BF16),
        pltpu.VMEM((REACH, CH * S, D), F32),
        pltpu.VMEM((REACH, CH, B, D), F32),
        pltpu.VMEM((REACH, CH, B, D), BF16),
        pltpu.VMEM((REACH, CH, B, D), BF16),
        pltpu.VMEM((2, 2, REACH, B, D), BF16),
        pltpu.VMEM((2, 2, REACH, B, D), BF16),
        dma((2, 2, 2, REACH)), dma((2, 2, 2, REACH)),
        dma((2, REACH, 4)), dma((2, REACH, 4)),
        dma((R,)), dma((R,)),
        dma((Z,)), dma((Z,)), dma((2,)),
        dma((3, 2)), dma((3, 2)),
        dma((R,)), dma((R,)),
        dma((R,)), dma((R,)),
        dma((R,)), dma((R,)),
        dma((R,)), dma((R,)),
        dma((R,)), dma((R,)),
        dma((R,)), dma((R,)),
        dma((R,)), dma((R,)),
        dma((R,)), dma((R,)),
        dma((R,)), dma((R,)),
        dma((2,)), dma((Z,)), dma((Z,)),
        dma((R,)), dma((R,)), dma((2,)),
        dma((REACH,)), dma((REACH,)),
        dma((2, 2, REACH)), dma((2, 2, REACH)),
        dma((R,)), dma((R,)),
    ]
    input_grad, qdown_g, qup_g, odown_g, oup_g = pl.pallas_call(
        functools.partial(kernel, R, Z),
        out_shape=outs,
        in_specs=[vmem] * 14,
        out_specs=[vmem] * 5,
        scratch_shapes=scratch,
        compiler_params=pltpu.CompilerParams(
            collective_id=0, has_side_effects=True, vmem_limit_bytes=56 * 1024 * 1024),
        name="attention_backward",
    )(
        hidden, cotangent, importance, positions, segments, norm_gain, query_weight_matrix,
        query_down_factor.T, key_weight.T, value_weight_matrix.T, output_weight_matrix, out_up,
        output_down_factor.T, query_up_factor,
    )
    return input_grad, qdown_g.T, qup_g, odown_g.T, oup_g


def solution(mesh):
    placed = (
        P("col", "row"), P("col", "row"), P("col"), P("col"), P("col"), P("row"),
        P("row", "col"), P("row", "col"), P("row", "col"), P("col", "row"),
        P("row", None), P(None, "col"), P("col", None), P(None, "row"),
    )
    return jax.shard_map(
        per_device,
        mesh=mesh,
        in_specs=placed,
        out_specs=(P("col", "row"), P("row", None), P(None, "col"), P("col", None), P(None, "row")),
        check_vma=False,
    )
```

```python
import functools
import math

import jax
import jax.numpy as jnp
from jax import lax
from jax.experimental import pallas as pl
from jax.experimental.pallas import tpu as pltpu
from jax.sharding import PartitionSpec as P

MODEL_WIDTH = 16384
HEAD = 128
RANK = 64
GROUP = 4
EPS = 1e-05
CAP = 2.0
BASE = 500000.0
FILL = -1e30
SCALE = HEAD**-0.5
MESH = pl.DeviceIdType.MESH
F32 = jnp.float32
BF16 = jnp.bfloat16
REACH = 4
NEAR = 3
STEPS = 4


def nn(a, b):
    return lax.dot_general(a, b, (((1,), (0,)), ((), ())), preferred_element_type=F32)


def nt(a, b):
    return lax.dot_general(a, b, (((1,), (1,)), ((), ())), preferred_element_type=F32)


def tn(a, b):
    return lax.dot_general(a, b, (((0,), (0,)), ((), ())), preferred_element_type=F32)


def remote(src, dst, send, recv, device):
    return pltpu.make_async_remote_copy(
        src_ref=src, dst_ref=dst, send_sem=send, recv_sem=recv,
        device_id=device, device_id_type=MESH,
    )


def kernel(
    R, Z,
    hid, cot, imp, posn, segm, gain,
    wq_hbm, qdown_hbm, kw_hbm, vw_hbm, wo_hbm, oup_hbm, odown_hbm, qup_hbm,
    igrad, qdown_g, qup_g, odown_g, oup_g,
    wq, wo, oup, odown_t, qup, small,
    h_all, w_all, n_all, aux_all, kvt,
    ssq, part_w, rx_w, part_kv, rx_kv, part_q, rx_q, kvgrp, kvx, lowx, kvpart, kvrx,
    qg_all, kvg_all, att_all, dots,
    lown, lowz, low_all, gq, own, sib_out, sib_in, hop_out, hop_in,
    load, ring_s, ring_r, sib_s, sib_r, ssq_s, ssq_r, aux_s, aux_r, auxsib, kvt_s, kvt_r,
    rsw_s, rsw_r, rsk_s, rsk_r, rsq_s, rsq_r, grp_s, grp_r, kvx_s, kvx_r, lowx_s, lowx_r,
    kvp_s, kvp_r, qg_s, qg_r, kvg_s, kvg_r, att_s, att_r,
    lowp, lowz_s, lowz_r, low_s, low_r, lowsib, sg_s, sg_r, hop_s, hop_r, dot_s, dot_r,
):
    row = lax.axis_index("row")
    col = lax.axis_index("col")
    z = lax.div(col, 2)
    core = lax.rem(col, 2)
    B, D = hid.shape
    S = 2 * B
    T = S * Z
    H = wo_hbm.shape[0]
    heads = H // HEAD
    counts = {1: Z // 2, -1: Z - 1 - Z // 2}
    dirs = (1, -1)
    drains = []

    def zmod(v):
        return lax.rem(v + 2 * Z, Z)

    def at_z(v):
        return {"col": zmod(v) * 2 + core}

    sibling = {"col": z * 2 + 1 - core}
    pair = z + 1 - 2 * lax.rem(z, 2)

    def peer(k):
        return lax.rem(row + k, R)

    def each(n, f):
        def step(k, carry):
            f(k)
            return carry
        lax.fori_loop(1, n, step, 0)

    def start(cp):
        cp.start()
        drains.append(cp.wait_send)
        return cp

    def row_copy(src, dst, ss, rs, k):
        return remote(src, dst, ss.at[k], rs, {"row": peer(k)})

    def row_bcast(src, dst_all, ss, rs):
        def one(k):
            return row_copy(src, dst_all.at[row], ss, rs.at[row], k)
        each(R, lambda k: one(k).start())
        drains.append(lambda: each(R, lambda k: one(k).wait_send()))

    def row_recv(dst_all, rs, ss, k):
        s = peer(k)
        row_copy(dst_all.at[s], dst_all.at[s], ss, rs.at[s], k).wait_recv()

    def z_bcast(src, dst_of, ss, rs):
        def one(k):
            return remote(src, dst_of(z), ss.at[k], rs.at[z], at_z(z + k))
        each(Z, lambda k: one(k).start())
        drains.append(lambda: each(Z, lambda k: one(k).wait_send()))

    def z_recv(dst_of, ss, rs):
        def one(k):
            s = zmod(z + k)
            remote(dst_of(s), dst_of(s), ss.at[k], rs.at[s], at_z(z + k)).wait_recv()
        each(Z, one)

    loads = {}
    for i, (name, src, dst) in enumerate((
        ("oup", oup_hbm, oup), ("kw", kw_hbm, small.at[0]), ("vw", vw_hbm, small.at[1]),
        ("qd0", qdown_hbm.at[pl.ds(0, 32)], small.at[2]),
        ("qd1", qdown_hbm.at[pl.ds(32, 32)], small.at[3]),
        ("wo", wo_hbm, wo), ("wq", wq_hbm, wq), ("odown", odown_hbm, odown_t),
        ("qup", qup_hbm, qup),
    )):
        loads[name] = pltpu.make_async_copy(src, dst, load.at[i])

    def loaded(*names):
        for name in names:
            loads[name].wait()

    def flush():
        for wait in drains:
            wait()
        drains.clear()

    barrier = pltpu.get_barrier_semaphore()
    each(R, lambda k: pl.semaphore_signal(
        barrier, inc=1, device_id={"row": peer(k)}, device_id_type=MESH))
    each(Z, lambda k: pl.semaphore_signal(
        barrier, inc=1, device_id=at_z(z + k), device_id_type=MESH))
    pl.semaphore_signal(barrier, inc=1, device_id=sibling, device_id_type=MESH)
    pl.semaphore_signal(
        barrier, inc=1, device_id={"col": pair * 2 + 1 - core}, device_id_type=MESH)
    for cp in loads.values():
        cp.start()

    diagonal = (lax.broadcasted_iota(jnp.int32, (B, B), 0)
                == lax.broadcasted_iota(jnp.int32, (B, B), 1))

    def column(v):
        return jnp.sum(jnp.where(diagonal, v.reshape(1, B), 0.0), axis=1, keepdims=True)

    hf = hid[...].astype(F32)
    gf = gain[...].astype(F32).reshape(1, D)
    w_own = (cot[...].astype(F32)
             * column(jnp.minimum(imp[...].astype(F32), CAP))).astype(BF16)
    w_all[z, core] = w_own
    h_all[z, core] = hid[...]
    loaded("oup")
    ssq[row] = jnp.concatenate([
        jnp.broadcast_to(jnp.sum(hf * hf, axis=1, keepdims=True), (B, 128 - RANK)),
        nt(w_own, oup[...])], axis=1)
    member = lax.rem(col, GROUP)
    pl.semaphore_wait(barrier, R - 1 + Z - 1 + 2)

    arrays = (h_all, w_all)

    def length(d, ch):
        return NEAR if ch == 0 else counts[d] - NEAR

    def ring_send(a, d, ch, t):
        off = t if ch == 0 else (0 if t == 0 else NEAR + t)
        block = arrays[a].at[zmod(z - d * off), core]
        target = z + d * (NEAR + 1 if ch == 1 and t == 0 else 1)
        i = 0 if d == 1 else 1
        return start(remote(
            block, block, ring_s.at[a, i, ch, t], ring_r.at[a, i, ch, t], at_z(target)))

    halves = {}

    def sib_send(a, t, i, off):
        block = arrays[a].at[zmod(z + off), core]
        cp = start(remote(block, block, sib_s.at[a, t, i], sib_r.at[a, t, i], sibling))
        halves.setdefault((a, min(t, STEPS - 1)), []).append(cp)

    flying = {}
    for a in range(2):
        for ch in (1, 0):
            for d in dirs:
                if length(d, ch) > 0:
                    flying[a, d, ch] = ring_send(a, d, ch, 0)
    row_bcast(ssq.at[row], ssq, ssq_s, ssq_r)
    for a in range(2):
        sib_send(a, STEPS, 3, 0)

    def ring_step(t):
        came = []
        for a in range(2):
            i = 0
            for ch in (1, 0):
                for d in dirs:
                    if t >= length(d, ch):
                        continue
                    flying[a, d, ch].wait_recv()
                    if t + 1 < length(d, ch):
                        flying[a, d, ch] = ring_send(a, d, ch, t + 1)
                    came.append((a, t, i, -d * (t + 1 + (NEAR if ch else 0))))
                    i += 1
        for arrival in came:
            sib_send(*arrival)

    def chips_of(t):
        return [-d * (t + 1 + (NEAR if ch else 0))
                for ch in (1, 0) for d in dirs if t < length(d, ch)]

    groups = [chips_of(t) for t in range(STEPS - 1)]
    groups.append(chips_of(STEPS - 1) + chips_of(STEPS) + [0])

    ring_step(0)
    each(R, lambda k: row_recv(ssq, ssq_r, ssq_s, k))
    total = ssq[0]
    for i in range(1, R):
        total = total + ssq[i]
    inv_own = lax.rsqrt(total[:, 0:1] * (1.0 / MODEL_WIDTH) + EPS)
    lane = lax.broadcasted_iota(jnp.int32, (B, 128), 1)
    hi = inv_own.astype(BF16).astype(F32)
    mid = (inv_own - hi).astype(BF16).astype(F32)
    lo = inv_own - hi - mid
    p_own = posn[...]
    p_hi = lax.div(p_own, 64)
    tile = jnp.where(lane >= 128 - RANK, total, jnp.where(lane == 0, hi, jnp.where(
        lane == 1, mid, lo)))
    for i, v in ((3, p_hi), (4, p_own - p_hi * 64), (5, segm[...])):
        tile = jnp.where(lane == i, column(v.astype(F32)), tile)
    aux_all[z, core] = tile.astype(BF16)
    z_bcast(aux_all.at[z, core], lambda s: aux_all.at[s, core], aux_s, aux_r)

    def rs_copy(src, dst, ss, rs, p):
        return remote(src.at[p], dst.at[row], ss.at[p], rs.at[row], {"row": p})

    def rs_send(group, src, dst, ss, rs):
        n = len(group)
        for m in range(n):
            turn = lax.rem(row + m, n)
            delta = group[0]
            for i in range(1, n):
                delta = jnp.where(turn == i, group[i], delta)
            p = zmod(z + delta)

            @pl.when(p != row)
            def _():
                rs_copy(src, dst, ss, rs, p).start()

    def rs_drain(src, dst, ss, rs):
        drains.append(lambda: each(R, lambda k: rs_copy(src, dst, ss, rs, peer(k)).wait_send()))

    def rows_of(ref, group, width):
        return jnp.concatenate(
            [ref[zmod(z + o)].reshape(S, width) for o in group], axis=0)

    def store(ref, group, value, at=slice(None)):
        for i, o in enumerate(group):
            ref[zmod(z + o), :, at] = value[i * S:(i + 1) * S]

    def project_w(t):
        g = groups[t]
        for cp in halves[1, t]:
            cp.wait_recv()
        store(part_w, g, nt(rows_of(w_all, g, D), wo[...]).astype(BF16))
        rs_send(g, part_w, rx_w, rsw_s, rsw_r)

    def project_kv(t):
        g = groups[t]
        for cp in halves[0, t]:
            cp.wait_recv()
        ax = rows_of(aux_all, g, 128).astype(F32)
        h = rows_of(h_all, g, D).astype(F32)
        n = (h * (ax[:, 0:1] + ax[:, 1:2] + ax[:, 2:3]) * gf).astype(BF16)
        store(n_all, g, n)
        store(part_kv, g, nt(n, small[...].reshape(128, D)).astype(BF16))
        rs_send(g, part_kv, rx_kv, rsk_s, rsk_r)

    def project_q(t):
        g = groups[t]
        store(part_q, g, nn(rows_of(n_all, g, D), wq[...]).astype(BF16))
        rs_send(g, part_q, rx_q, rsq_s, rsq_r)

    ring_step(1)
    loaded("wo")
    project_w(0)
    ring_step(2)
    z_recv(lambda s: aux_all.at[s, core], aux_s, aux_r)
    aux_half = start(remote(
        aux_all.at[:, core], aux_all.at[:, core], auxsib.at[0], auxsib.at[1], sibling))
    project_w(1)
    loaded("kw", "vw", "qd0", "qd1", "wq")
    aux_half.wait_recv()
    project_kv(0)
    project_q(0)
    ring_step(3)
    project_kv(1)
    project_q(1)
    project_w(2)
    ring_step(4)
    project_kv(2)
    project_kv(3)
    project_q(2)
    project_q(3)
    project_w(3)
    kvt[:, member] = small[0:2]
    kvt_own = kvt.at[:, member]
    kvt_sib = start(remote(kvt_own, kvt_own, kvt_s.at[0], kvt_r.at[0], sibling))
    kvt_pair = start(remote(
        kvt_own, kvt_own, kvt_s.at[1], kvt_r.at[1], {"col": pair * 2 + core}))
    rs_drain(part_w, rx_w, rsw_s, rsw_r)
    rs_drain(part_kv, rx_kv, rsk_s, rsk_r)
    rs_drain(part_q, rx_q, rsq_s, rsq_r)

    ax = aux_all[row].reshape(S, 128).astype(F32)
    pos = ax[:, 3:4] * 64.0 + ax[:, 4:5]
    lane_s = lax.broadcasted_iota(jnp.int32, (S, HEAD), 1)
    half_lane = lax.rem(lane_s, HEAD // 2).astype(F32)
    angle = pos * jnp.exp(half_lane * (-2.0 * math.log(BASE) / HEAD))
    cosine = jnp.cos(angle)
    sine = jnp.where(lane_s < HEAD // 2, -1.0, 1.0) * jnp.sin(angle)

    def swap(x):
        return jnp.concatenate([x[:, HEAD // 2:], x[:, :HEAD // 2]], axis=1)

    def rotate(x):
        return x * cosine + swap(x) * sine

    def unrotate(x):
        return x * cosine - swap(x) * sine

    pick = (lax.broadcasted_iota(jnp.int32, (8, 128), 1) == 5).astype(BF16)
    seg_key = nt(pick, aux_all[...].reshape(T, 128))[0:1, :]
    token = row * S + lax.broadcasted_iota(jnp.int32, (S, T), 0)
    allowed = (ax[:, 5:6] == seg_key) & (lax.broadcasted_iota(jnp.int32, (S, T), 1) <= token)
    allowed = jnp.concatenate([allowed.astype(F32)] * heads, axis=0) > 0.5

    def rs_sum(part, rx, ss, rs):
        acc = part[row].astype(F32)
        for k in range(1, R):
            row_recv(rx, rs, ss, k)
            acc = acc + rx[peer(k)].astype(F32)
        return acc

    kvl = rs_sum(part_kv, rx_kv, rsk_s, rsk_r)
    kvgrp[member] = kvl
    kvl_cp = []
    for i, dev in enumerate((sibling, {"col": pair * 2 + core}, {"col": pair * 2 + 1 - core})):
        kvl_cp.append(start(remote(
            kvgrp.at[member], kvgrp.at[member], grp_s.at[i], grp_r.at[i], dev)))
    low = kvl.astype(BF16)
    lowx[row] = low
    loaded("qup", "odown")
    ql = 2.0 * nn(low[:, RANK:2 * RANK], qup[...])
    dA = 2.0 * nn(aux_all[row].reshape(S, 128)[:, 128 - RANK:128], odown_t[...])
    for cp in kvl_cp:
        cp.wait_recv()
    part = HEAD // GROUP
    kl, vl = (jnp.concatenate(
        [kvgrp[g][:, half * part:(half + 1) * part] for g in range(GROUP)], axis=1)
        for half in range(2))
    kvx[row, :, 0:HEAD] = rotate(kl).astype(BF16)
    kvx[row, :, HEAD:2 * HEAD] = vl.astype(BF16)
    row_bcast(kvx.at[row], kvx, kvx_s, kvx_r)
    ql = ql + rs_sum(part_q, rx_q, rsq_s, rsq_r)
    queries = jnp.concatenate(
        [rotate(ql[:, i * HEAD:(i + 1) * HEAD]).astype(BF16) for i in range(heads)], axis=0)
    each(R, lambda k: row_recv(kvx, kvx_r, kvx_s, k))

    keys = kvx[:, :, 0:HEAD].reshape(T, HEAD)
    values = kvx[:, :, HEAD:2 * HEAD].reshape(T, HEAD)
    scores = jnp.where(allowed, nt(queries, keys) * SCALE, FILL)
    shifted = jnp.exp(scores - jnp.max(scores, axis=1, keepdims=True))
    probs = shifted / jnp.sum(shifted, axis=1, keepdims=True)
    narrow = probs.astype(BF16)
    dA = (dA + rs_sum(part_w, rx_w, rsw_s, rsw_r)).astype(BF16)
    grads = jnp.concatenate([dA[:, i * HEAD:(i + 1) * HEAD] for i in range(heads)], axis=0)
    pgrad = nt(grads, values)
    rdot = jnp.sum(probs * pgrad, axis=1, keepdims=True)
    sgrad = (probs * (pgrad - rdot) * SCALE).astype(BF16)
    kvpart[:, :, 0:HEAD] = tn(sgrad, queries).astype(BF16).reshape(R, S, HEAD)
    kvpart[:, :, HEAD:2 * HEAD] = tn(narrow, grads).astype(BF16).reshape(R, S, HEAD)

    def kvp_copy(k):
        return remote(kvpart.at[peer(k)], kvrx.at[row], kvp_s.at[k], kvp_r.at[row],
                      {"row": peer(k)})

    each(R, lambda k: kvp_copy(k).start())
    drains.append(lambda: each(R, lambda k: kvp_copy(k).wait_send()))
    qg = nn(sgrad, keys)
    for i in range(heads):
        qg_all[row, :, i * HEAD:(i + 1) * HEAD] = unrotate(qg[i * S:(i + 1) * S]).astype(BF16)
    row_bcast(qg_all.at[row], qg_all, qg_s, qg_r)
    att = nn(narrow, values).astype(BF16)
    for i in range(heads):
        att_all[row, :, i * HEAD:(i + 1) * HEAD] = att[i * S:(i + 1) * S]

    inner = jnp.concatenate(
        [nt(att_all[row], odown_t[...]), nt(qg_all[row], qup[...])], axis=1)
    lown[0] = jnp.where(core == 0, inner[0:B], inner[B:S])
    lown[1] = jnp.where(core == 0, inner[B:S], inner[0:B])
    low_pair = start(remote(lown.at[1], lown.at[2], lowp.at[0], lowp.at[1], sibling))
    kvt_pair.wait_recv()
    other = kvt.at[:, 2 * lax.rem(pair, 2) + core]
    kvt_other = start(remote(other, other, kvt_s.at[2], kvt_r.at[2], sibling))
    kacc = rs_sum(kvpart, kvrx, kvp_s, kvp_r)
    kvg_all[row, :, 0:HEAD] = unrotate(kacc[:, 0:HEAD]).astype(BF16)
    kvg_all[row, :, HEAD:2 * HEAD] = kacc[:, HEAD:2 * HEAD].astype(BF16)
    row_bcast(kvg_all.at[row], kvg_all, kvg_s, kvg_r)
    low_pair.wait_recv()
    lowz[z] = lown[0] + lown[2]
    z_bcast(lowz.at[z], lambda s: lowz.at[s], lowz_s, lowz_r)
    row_bcast(lowx.at[row], lowx, lowx_s, lowx_r)
    row_bcast(att_all.at[row], att_all, att_s, att_r)

    each(R, lambda k: row_recv(qg_all, qg_r, qg_s, k))
    order = list(reversed(range(REACH)))

    def hop_length(d, ch):
        return REACH if ch == 0 else counts[d] - REACH

    bgroups = [[-d * (t + 1 + (REACH if ch else 0))
                for ch in (1, 0) for d in dirs if t < hop_length(d, ch)] for t in range(REACH)]
    bgroups[REACH - 1].append(0)
    for t in order:
        gq[t, 0:len(bgroups[t]) * S] = nt(rows_of(qg_all, bgroups[t], H), wq[...])
    z_recv(lambda s: lowz.at[s], lowz_s, lowz_r)
    inner = lowz[0]
    for i in range(1, Z):
        inner = inner + lowz[i]
    low_all[row, core] = inner.astype(BF16)
    row_bcast(low_all.at[row, core], low_all.at[:, core], low_s, low_r)
    each(R, lambda k: row_recv(kvg_all, kvg_r, kvg_s, k))
    kvt_sib.wait_recv()
    kvt_other.wait_recv()

    def backward(t):
        g = bgroups[t]
        value = gq[t, 0:len(g) * S] + nn(
            rows_of(kvg_all, g, 2 * HEAD), kvt[...].reshape(2 * HEAD, D))
        value = value.reshape(len(g), 2, B, D)
        mine = core == 0
        sib_out[t, 0:len(g)] = jnp.where(mine, value[:, 1], value[:, 0]).astype(BF16)
        cp = start(remote(sib_out.at[t, pl.ds(0, len(g))], sib_in.at[t, pl.ds(0, len(g))],
                          sg_s.at[t], sg_r.at[t], sibling))
        own[t, 0:len(g)] = jnp.where(mine, value[:, 0], value[:, 1])
        return cp

    hops = {}

    def hop(d, ch, t):
        i = 0 if d == 1 else 1
        far = ch == 1 and t == REACH - 1
        return remote(hop_out.at[i, ch, t], hop_in.at[i, ch, t], hop_s.at[i, ch, t],
                      hop_r.at[i, ch, t], at_z(z + d * (REACH + 1 if far else 1)))

    def hop_step(t, cp):
        u = REACH - 1 - t
        cp.wait_recv()
        for ch in (1, 0):
            for d in dirs:
                delta = u + 1 + (REACH if ch else 0)
                last = REACH if ch == 0 else counts[d]
                if delta > last:
                    continue
                i = 0 if d == 1 else 1
                slot = bgroups[u].index(d * delta if d * delta in bgroups[u] else -d * delta)
                term = own[u, slot] + sib_in[u, slot].astype(F32)
                if delta < last:
                    hops[d, ch, t - 1].wait_recv()
                    term = term + hop_in[i, ch, t - 1].astype(F32)
                hop_out[i, ch, t] = term.astype(BF16)
                hops[d, ch, t] = start(hop(d, ch, t))

    sibs = {}
    for t, u in enumerate(order):
        sibs[t] = backward(u)
        if t > 0:
            hop_step(t - 1, sibs[t - 1])
    own_slot = bgroups[REACH - 1].index(0)
    final = own[REACH - 1, own_slot] + sib_in[REACH - 1, own_slot].astype(F32)
    low_all_row = low_all.at[:, core]
    each(R, lambda k: row_recv(low_all_row, low_r, low_s, k))
    low_half = start(remote(low_all_row, low_all_row, lowsib.at[0], lowsib.at[1], sibling))
    hop_step(REACH - 1, sibs[REACH - 1])
    each(R, lambda k: row_recv(lowx, lowx_r, lowx_s, k))
    lows_all = lowx[...].reshape(T, 128)
    qup_g[...] = 2.0 * tn(lows_all, qg_all[...].reshape(T, H))[RANK:2 * RANK]
    flush()
    low_half.wait_recv()
    lb = low_all[...].reshape(T, 128)
    oup_g[...] = 2.0 * tn(lb, w_all[...].reshape(T, D))[0:RANK]
    qdown_g[...] = 2.0 * tn(lb, n_all[...].reshape(T, D))[RANK:2 * RANK]
    low_back = low_all[z, core][:, RANK:2 * RANK]
    final = final + 2.0 * nn(low_back, small[2:4].reshape(RANK, D))
    for ch in (0, 1):
        for d in dirs:
            if hop_length(d, ch) > 0:
                hops[d, ch, REACH - 1].wait_recv()
                final = final + hop_in[0 if d == 1 else 1, ch, REACH - 1].astype(F32)
    dots[row] = jnp.broadcast_to(
        jnp.sum(hf * gf * final, axis=1, keepdims=True), (B, 128))
    row_bcast(dots.at[row], dots, dot_s, dot_r)
    each(R, lambda k: row_recv(att_all, att_r, att_s, k))
    odown_g[...] = 2.0 * tn(aux_all[...].reshape(T, 128), att_all[...].reshape(T, H))[128 - RANK:128]
    inv = inv_own
    flush()
    base = w_own.astype(F32) + inv * gf * final
    each(R, lambda k: row_recv(dots, dot_r, dot_s, k))
    dsum = dots[0]
    for i in range(1, R):
        dsum = dsum + dots[i]
    igrad[...] = base - hf * (inv * inv * inv * dsum[:, 0:1] * (1.0 / MODEL_WIDTH))

    flush()


def finish(*refs):
    n = len(refs) // 2
    for i in range(n):
        refs[n + i][...] = refs[i][...]


def per_device(
    hidden, cotangent, importance, positions, segments, norm_gain, query_weight_matrix,
    key_weight, value_weight_matrix, output_weight_matrix, query_down_factor, query_up_factor,
    output_down_factor, out_up,
):
    R = lax.axis_size("row")
    C = lax.axis_size("col")
    Z = C // 2
    B, D = hidden.shape
    H = query_weight_matrix.shape[1]
    S = 2 * B
    CH = Z // REACH
    vmem = pl.BlockSpec(memory_space=pltpu.VMEM)
    dma = pltpu.SemaphoreType.DMA
    outs = (
        jax.ShapeDtypeStruct((B, D), F32),
        jax.ShapeDtypeStruct((RANK, D), F32),
        jax.ShapeDtypeStruct((RANK, H), F32),
        jax.ShapeDtypeStruct((RANK, H), F32),
        jax.ShapeDtypeStruct((RANK, D), F32),
    )
    scratch = [
        pltpu.VMEM((D, H), BF16),
        pltpu.VMEM((H, D), BF16),
        pltpu.VMEM((RANK, D), BF16),
        pltpu.VMEM((RANK, H), BF16),
        pltpu.VMEM((RANK, H), BF16),
        pltpu.VMEM((4, 32, D), BF16),
        pltpu.VMEM((Z, 2, B, D), BF16),
        pltpu.VMEM((Z, 2, B, D), BF16),
        pltpu.VMEM((Z, S, D), BF16),
        pltpu.VMEM((Z, 2, B, 128), BF16),
        pltpu.VMEM((2, GROUP, HEAD // GROUP, D), BF16),
        pltpu.VMEM((R, B, 128), F32),
        pltpu.VMEM((R, S, H), BF16),
        pltpu.VMEM((R, S, H), BF16),
        pltpu.VMEM((R, S, HEAD), BF16),
        pltpu.VMEM((R, S, HEAD), BF16),
        pltpu.VMEM((R, S, H), BF16),
        pltpu.VMEM((R, S, H), BF16),
        pltpu.VMEM((GROUP, S, HEAD), F32),
        pltpu.VMEM((R, S, 2 * HEAD), BF16),
        pltpu.VMEM((R, S, 128), BF16),
        pltpu.VMEM((R, S, 2 * HEAD), BF16),
        pltpu.VMEM((R, S, 2 * HEAD), BF16),
        pltpu.VMEM((R, S, H), BF16),
        pltpu.VMEM((R, S, 2 * HEAD), BF16),
        pltpu.VMEM((R, S, H), BF16),
        pltpu.VMEM((R, B, 128), F32),
        pltpu.VMEM((3, B, 128), F32),
        pltpu.VMEM((Z, B, 128), F32),
        pltpu.VMEM((R, 2, B, 128), BF16),
        pltpu.VMEM((REACH, CH * S, D), F32),
        pltpu.VMEM((REACH, CH, B, D), F32),
        pltpu.VMEM((REACH, CH, B, D), BF16),
        pltpu.VMEM((REACH, CH, B, D), BF16),
        pltpu.VMEM((2, 2, REACH, B, D), BF16),
        pltpu.VMEM((2, 2, REACH, B, D), BF16),
        dma((9,)),
        dma((2, 2, 2, 8)), dma((2, 2, 2, 8)),
        dma((2, 8, 4)), dma((2, 8, 4)),
        dma((R,)), dma((R,)),
        dma((Z,)), dma((Z,)), dma((2,)),
        dma((3,)), dma((3,)),
        dma((R,)), dma((R,)),
        dma((R,)), dma((R,)),
        dma((R,)), dma((R,)),
        dma((3,)), dma((3,)),
        dma((R,)), dma((R,)),
        dma((R,)), dma((R,)),
        dma((R,)), dma((R,)),
        dma((R,)), dma((R,)),
        dma((R,)), dma((R,)),
        dma((R,)), dma((R,)),
        dma((2,)), dma((Z,)), dma((Z,)),
        dma((R,)), dma((R,)), dma((2,)),
        dma((REACH,)), dma((REACH,)),
        dma((2, 2, REACH)), dma((2, 2, REACH)),
        dma((R,)), dma((R,)),
    ]
    results = pl.pallas_call(
        functools.partial(kernel, R, Z),
        out_shape=outs,
        in_specs=[vmem] * 6 + [pl.BlockSpec(memory_space=pl.ANY)] * 8,
        out_specs=[vmem] * 5,
        scratch_shapes=scratch,
        compiler_params=pltpu.CompilerParams(
            collective_id=0, has_side_effects=True, vmem_limit_bytes=56 * 1024 * 1024),
        name="attention_backward",
    )(
        hidden, cotangent, importance, positions, segments, norm_gain, query_weight_matrix,
        query_down_factor.T, key_weight.T, value_weight_matrix.T, output_weight_matrix, out_up,
        output_down_factor.T, query_up_factor,
    )
    input_grad, qdown_g, qup_g, odown_g, oup_g = pl.pallas_call(
        finish,
        out_shape=outs,
        in_specs=[vmem] * 5,
        out_specs=[vmem] * 5,
        name="place_results",
    )(*results)
    return input_grad, qdown_g.T, qup_g, odown_g.T, oup_g


def solution(mesh):
    placed = (
        P("col", "row"), P("col", "row"), P("col"), P("col"), P("col"), P("row"),
        P("row", "col"), P("row", "col"), P("row", "col"), P("col", "row"),
        P("row", None), P(None, "col"), P("col", None), P(None, "row"),
    )
    return jax.shard_map(
        per_device,
        mesh=mesh,
        in_specs=placed,
        out_specs=(P("col", "row"), P("row", None), P(None, "col"), P("col", None), P(None, "row")),
        check_vma=False,
    )
```

```python
import functools
import math

import jax
import jax.numpy as jnp
from jax import lax
from jax.experimental import pallas as pl
from jax.experimental.pallas import tpu as pltpu
from jax.sharding import PartitionSpec as P

MODEL_WIDTH = 16384
HEAD = 128
RANK = 64
GROUP = 4
EPS = 1e-05
CAP = 2.0
BASE = 500000.0
FILL = -1e30
SCALE = HEAD**-0.5
MESH = pl.DeviceIdType.MESH
F32 = jnp.float32
BF16 = jnp.bfloat16
REACH = 4
NEAR = 4
STEPS = 4
SHIFT = 3


def nn(a, b):
    return lax.dot_general(a, b, (((1,), (0,)), ((), ())), preferred_element_type=F32)


def nt(a, b):
    return lax.dot_general(a, b, (((1,), (1,)), ((), ())), preferred_element_type=F32)


def tn(a, b):
    return lax.dot_general(a, b, (((0,), (0,)), ((), ())), preferred_element_type=F32)


def remote(src, dst, send, recv, device):
    return pltpu.make_async_remote_copy(
        src_ref=src, dst_ref=dst, send_sem=send, recv_sem=recv,
        device_id=device, device_id_type=MESH,
    )


def kernel(
    R, Z,
    hid, cot, imp, posn, segm, gain,
    wq_hbm, qdown_hbm, kw_hbm, vw_hbm, wo_hbm, oup_hbm, odown_hbm, qup_hbm,
    igrad, qdown_g, qup_g, odown_g, oup_g,
    wq, wo, oup, odown_t, qup, small,
    h_all, w_all, n_all, aux_all, kvt,
    ssq, part_w, rx_w, part_h, rx_h, aux_s, low_nat, kvgrp, kvx, lowx, kvpart, kvrx,
    qg_all, kvg_all, att_all, dots,
    lown, lowz, low_all, gq, own, sib_out, sib_in, hop_out, hop_in,
    load, ring_s, ring_r, sib_s, sib_r, ssq_s, ssq_r, auxz_s, auxz_r, auxsib, kvt_s, kvt_r,
    rsw_s, rsw_r, rsh_s, rsh_r, grp_s, grp_r, kvx_s, kvx_r, lowx_s, lowx_r,
    kvp_s, kvp_r, qg_s, qg_r, kvg_s, kvg_r, att_s, att_r,
    lowp, lowz_s, lowz_r, low_s, low_r, lowsib, sg_s, sg_r, hop_s, hop_r, dot_s, dot_r,
):
    row = lax.axis_index("row")
    col = lax.axis_index("col")
    z = lax.div(col, 2)
    core = lax.rem(col, 2)
    B, D = hid.shape
    S = 2 * B
    T = S * Z
    H = wo_hbm.shape[0]
    heads = H // HEAD
    counts = {1: Z // 2, -1: Z - 1 - Z // 2}
    dirs = (1, -1)
    drains = []

    def zmod(v):
        return lax.rem(v + 2 * Z, Z)

    def at_z(v):
        return {"col": zmod(v) * 2 + core}

    sibling = {"col": z * 2 + 1 - core}
    pair = z + 1 - 2 * lax.rem(z, 2)

    def peer(k):
        return lax.rem(row + k, R)

    def each(n, f):
        for k in range(1, n):
            f(k)

    def start(cp):
        cp.start()
        drains.append(cp.wait_send)
        return cp

    def every(ref, ss, rs, device):
        most = ref.at[pl.ds(0, R - 1)]
        return remote(most, most, ss.at[0], rs.at[0], device)

    def row_bcast(src, dst_all, ss, rs):
        each(R, lambda k: remote(
            src, dst_all.at[row], ss.at[0], rs.at[0], {"row": peer(k)}).start())
        drains.append(lambda: every(dst_all, ss, rs, {"row": peer(1)}).wait_send())

    def row_recv(dst_all, rs, ss):
        every(dst_all, ss, rs, {"row": peer(1)}).wait_recv()

    def z_bcast(src, dst_all, ss, rs):
        each(Z, lambda k: remote(
            src, dst_all.at[z], ss.at[0], rs.at[0], at_z(z + k)).start())
        drains.append(lambda: every(dst_all, ss, rs, at_z(z + 1)).wait_send())

    def z_recv(dst_all, ss, rs):
        every(dst_all, ss, rs, at_z(z + 1)).wait_recv()

    loads = {}
    for i, (name, src, dst) in enumerate((
        ("oup", oup_hbm, oup), ("kw", kw_hbm, small.at[0]), ("vw", vw_hbm, small.at[1]),
        ("qd0", qdown_hbm.at[pl.ds(0, 32)], small.at[2]),
        ("qd1", qdown_hbm.at[pl.ds(32, 32)], small.at[3]),
        ("wo", wo_hbm, wo), ("wq", wq_hbm, wq), ("odown", odown_hbm, odown_t),
        ("qup", qup_hbm, qup),
    )):
        loads[name] = pltpu.make_async_copy(src, dst, load.at[i])

    def loaded(*names):
        for name in names:
            loads[name].wait()

    def flush():
        for wait in drains:
            wait()
        drains.clear()

    barrier = pltpu.get_barrier_semaphore()
    each(R, lambda k: pl.semaphore_signal(
        barrier, inc=1, device_id={"row": peer(k)}, device_id_type=MESH))
    each(Z, lambda k: pl.semaphore_signal(
        barrier, inc=1, device_id=at_z(z + k), device_id_type=MESH))
    pl.semaphore_signal(barrier, inc=1, device_id=sibling, device_id_type=MESH)
    pl.semaphore_signal(
        barrier, inc=1, device_id={"col": pair * 2 + 1 - core}, device_id_type=MESH)
    for cp in loads.values():
        cp.start()

    diagonal = (lax.broadcasted_iota(jnp.int32, (B, B), 0)
                == lax.broadcasted_iota(jnp.int32, (B, B), 1))

    def column(v):
        return jnp.sum(jnp.where(diagonal, v.reshape(1, B), 0.0), axis=1, keepdims=True)

    hf = hid[...].astype(F32)
    gf = gain[...].astype(F32).reshape(1, D)
    w_own = (cot[...].astype(F32)
             * column(jnp.minimum(imp[...].astype(F32), CAP))).astype(BF16)
    w_all[z, core] = w_own
    h_all[z, core] = hid[...]
    loaded("oup")
    ssq[row] = jnp.concatenate([
        jnp.broadcast_to(jnp.sum(hf * hf, axis=1, keepdims=True), (B, 128 - RANK)),
        nt(w_own, oup[...])], axis=1)
    member = lax.rem(col, GROUP)
    pl.semaphore_wait(barrier, R - 1 + Z - 1 + 2)

    arrays = (h_all, w_all)

    def length(d, ch):
        return NEAR if ch == 0 else counts[d] - NEAR

    def ring_send(a, d, ch, t):
        off = t if ch == 0 else (0 if t == 0 else NEAR + t)
        block = arrays[a].at[zmod(z - d * off), core]
        target = z + d * (NEAR + 1 if ch == 1 and t == 0 else 1)
        i = 0 if d == 1 else 1
        return start(remote(
            block, block, ring_s.at[a, i, ch, t], ring_r.at[a, i, ch, t], at_z(target)))

    halves = {}

    def sib_send(a, t, i, off):
        block = arrays[a].at[zmod(z + off), core]
        cp = start(remote(block, block, sib_s.at[a, t, i], sib_r.at[a, t, i], sibling))
        halves.setdefault((a, min(t, STEPS - 1)), []).append(cp)

    flying = {}
    for a in range(2):
        for ch in (1, 0):
            for d in dirs:
                if length(d, ch) > 0:
                    flying[a, d, ch] = ring_send(a, d, ch, 0)
    row_bcast(ssq.at[row], ssq, ssq_s, ssq_r)
    for a in range(2):
        sib_send(a, STEPS, 3, 0)

    def ring_step(t):
        came = []
        for a in range(2):
            i = 0
            for ch in (1, 0):
                for d in dirs:
                    if t >= length(d, ch):
                        continue
                    flying[a, d, ch].wait_recv()
                    if t + 1 < length(d, ch):
                        flying[a, d, ch] = ring_send(a, d, ch, t + 1)
                    came.append((a, t, i, -d * (t + 1 + (NEAR if ch else 0))))
                    i += 1
        for arrival in came:
            sib_send(*arrival)

    def chips_of(t):
        return [-d * (t + 1 + (NEAR if ch else 0))
                for ch in (1, 0) for d in dirs if t < length(d, ch)]

    groups = [chips_of(t) for t in range(STEPS - 1)]
    groups.append(chips_of(STEPS - 1) + chips_of(STEPS) + [0])

    def slice_of(o, b):
        return zmod(z + o + SHIFT * b), b

    slices = {(c, b): ((c + SHIFT * b) % Z, b) for c in range(Z) for b in range(2)}

    ring_step(0)
    row_recv(ssq, ssq_r, ssq_s)
    total = ssq[0]
    for i in range(1, R):
        total = total + ssq[i]
    inv_own = lax.rsqrt(total[:, 0:1] * (1.0 / MODEL_WIDTH) + EPS)
    lane = lax.broadcasted_iota(jnp.int32, (B, 128), 1)
    hi = inv_own.astype(BF16).astype(F32)
    mid = (inv_own - hi).astype(BF16).astype(F32)
    lo = inv_own - hi - mid
    p_own = posn[...]
    p_hi = lax.div(p_own, 64)
    tile = jnp.where(lane >= 128 - RANK, total, jnp.where(lane == 0, hi, jnp.where(
        lane == 1, mid, lo)))
    for i, v in ((3, p_hi), (4, p_own - p_hi * 64), (5, segm[...])):
        tile = jnp.where(lane == i, column(v.astype(F32)), tile)
    tile = jnp.where(lane == 6, col.astype(F32), tile)
    tile = jnp.where(
        lane == 7, lax.broadcasted_iota(jnp.int32, (B, 128), 0).astype(F32), tile)
    aux_all[z, core] = tile.astype(BF16)
    z_bcast(aux_all.at[z, core], aux_all.at[:, core], auxz_s, auxz_r)

    def rs_send(gi, src, dst, ss, rs):
        for b in range(2):
            for o in groups[gi]:
                p = zmod(z + o + SHIFT * b)

                @pl.when(p != row)
                def _():
                    remote(src.at[p, b], dst.at[row, b], ss.at[0], rs.at[0], {"row": p}).start()

    def rs_drain(src, ss, rs):
        drains.append(lambda: every(src, ss, rs, {"row": peer(1)}).wait_send())

    def rows_of(ref, group, width):
        return jnp.concatenate(
            [ref[zmod(z + o)].reshape(S, width) for o in group], axis=0)

    def store(ref, group, value, at):
        for i, o in enumerate(group):
            for b in range(2):
                r, half = slice_of(o, b)
                ref[r, half, :, at] = value[i * S + b * B:i * S + (b + 1) * B]

    def project_w(t):
        g = groups[t]
        for cp in halves[1, t]:
            cp.wait_recv()
        store(part_w, g, nt(rows_of(w_all, g, D), wo[...]).astype(BF16), slice(0, H))
        rs_send(t, part_w, rx_w, rsw_s, rsw_r)

    def project_h(t):
        g = groups[t]
        for cp in halves[0, t]:
            cp.wait_recv()
        ax = rows_of(aux_all, g, 128).astype(F32)
        h = rows_of(h_all, g, D).astype(F32)
        n = (h * (ax[:, 0:1] + ax[:, 1:2] + ax[:, 2:3]) * gf).astype(BF16)
        for i, o in enumerate(g):
            n_all[zmod(z + o)] = n[i * S:(i + 1) * S]
        store(part_h, g, nt(n, small[...].reshape(128, D)).astype(BF16), slice(H, H + 128))
        store(part_h, g, nn(n, wq[...]).astype(BF16), slice(0, H))
        rs_send(t, part_h, rx_h, rsh_s, rsh_r)

    ring_step(1)
    loaded("wo")
    project_w(0)
    ring_step(2)
    z_recv(aux_all.at[:, core], auxz_s, auxz_r)
    aux_half = start(remote(
        aux_all.at[:, core], aux_all.at[:, core], auxsib.at[0], auxsib.at[1], sibling))
    project_w(1)
    loaded("kw", "vw", "qd0", "qd1", "wq")
    aux_half.wait_recv()
    project_h(0)
    ring_step(3)
    project_h(1)
    project_w(2)
    ring_step(4)
    project_h(2)
    project_h(3)
    project_w(3)
    kvt[:, member] = small[0:2]
    kvt_own = kvt.at[:, member]
    kvt_sib = start(remote(kvt_own, kvt_own, kvt_s.at[0], kvt_r.at[0], sibling))
    kvt_pair = start(remote(
        kvt_own, kvt_own, kvt_s.at[1], kvt_r.at[1], {"col": pair * 2 + core}))
    rs_drain(part_w, rsw_s, rsw_r)
    rs_drain(part_h, rsh_s, rsh_r)

    for (o, b), (r, half) in slices.items():
        aux_s[r, half] = aux_all[o, b]
    ax = aux_s[row].reshape(S, 128).astype(F32)
    pos = ax[:, 3:4] * 64.0 + ax[:, 4:5]
    lane_s = lax.broadcasted_iota(jnp.int32, (S, HEAD), 1)
    half_lane = lax.rem(lane_s, HEAD // 2).astype(F32)
    angle = pos * jnp.exp(half_lane * (-2.0 * math.log(BASE) / HEAD))
    cosine = jnp.cos(angle)
    sine = jnp.where(lane_s < HEAD // 2, -1.0, 1.0) * jnp.sin(angle)

    def swap(x):
        return jnp.concatenate([x[:, HEAD // 2:], x[:, :HEAD // 2]], axis=1)

    def rotate(x):
        return x * cosine + swap(x) * sine

    def unrotate(x):
        return x * cosine - swap(x) * sine

    pick_row = lax.broadcasted_iota(jnp.int32, (8, 128), 0)
    pick_lane = lax.broadcasted_iota(jnp.int32, (8, 128), 1)
    pick = jnp.where(pick_row == 0, (pick_lane == 5).astype(F32), jnp.where(
        pick_row == 1, jnp.where(pick_lane == 6, float(B), (pick_lane == 7).astype(F32)), 0.0))
    of_key = nt(pick.astype(BF16), aux_s[...].reshape(T, 128))
    token = ax[:, 6:7] * float(B) + ax[:, 7:8]
    allowed = (ax[:, 5:6] == of_key[0:1, :]) & (of_key[1:2, :] <= token)
    allowed = jnp.concatenate([allowed.astype(F32)] * heads, axis=0) > 0.5

    def rs_sum(part, rx, ss, rs, width):
        row_recv(rx, rs, ss)
        acc = part[row].reshape(S, width).astype(F32)
        for k in range(1, R):
            acc = acc + rx[peer(k)].reshape(S, width).astype(F32)
        return acc

    summed = rs_sum(part_h, rx_h, rsh_s, rsh_r, H + 128)
    kvl = summed[:, H:H + 128]
    kvgrp[member] = kvl
    kvl_cp = []
    for i, dev in enumerate((sibling, {"col": pair * 2 + core}, {"col": pair * 2 + 1 - core})):
        kvl_cp.append(start(remote(
            kvgrp.at[member], kvgrp.at[member], grp_s.at[i], grp_r.at[i], dev)))
    low = kvl.astype(BF16)
    lowx[row] = low
    loaded("qup", "odown")
    ql = 2.0 * nn(low[:, RANK:2 * RANK], qup[...])
    dA = 2.0 * nn(aux_s[row].reshape(S, 128)[:, 128 - RANK:128], odown_t[...])
    for cp in kvl_cp:
        cp.wait_recv()
    part = HEAD // GROUP
    kl, vl = (jnp.concatenate(
        [kvgrp[g][:, half * part:(half + 1) * part] for g in range(GROUP)], axis=1)
        for half in range(2))
    kvx[row, :, 0:HEAD] = rotate(kl).astype(BF16)
    kvx[row, :, HEAD:2 * HEAD] = vl.astype(BF16)
    row_bcast(kvx.at[row], kvx, kvx_s, kvx_r)
    ql = ql + summed[:, 0:H]
    queries = jnp.concatenate(
        [rotate(ql[:, i * HEAD:(i + 1) * HEAD]).astype(BF16) for i in range(heads)], axis=0)
    row_recv(kvx, kvx_r, kvx_s)

    keys = kvx[:, :, 0:HEAD].reshape(T, HEAD)
    values = kvx[:, :, HEAD:2 * HEAD].reshape(T, HEAD)
    scores = jnp.where(allowed, nt(queries, keys) * SCALE, FILL)
    shifted = jnp.exp(scores - jnp.max(scores, axis=1, keepdims=True))
    probs = shifted / jnp.sum(shifted, axis=1, keepdims=True)
    narrow = probs.astype(BF16)
    dA = (dA + rs_sum(part_w, rx_w, rsw_s, rsw_r, H)).astype(BF16)
    grads = jnp.concatenate([dA[:, i * HEAD:(i + 1) * HEAD] for i in range(heads)], axis=0)
    pgrad = nt(grads, values)
    rdot = jnp.sum(probs * pgrad, axis=1, keepdims=True)
    sgrad = (probs * (pgrad - rdot) * SCALE).astype(BF16)
    kvpart[:, :, 0:HEAD] = tn(sgrad, queries).astype(BF16).reshape(R, S, HEAD)
    kvpart[:, :, HEAD:2 * HEAD] = tn(narrow, grads).astype(BF16).reshape(R, S, HEAD)

    each(R, lambda k: remote(
        kvpart.at[peer(k)], kvrx.at[row], kvp_s.at[0], kvp_r.at[0], {"row": peer(k)}).start())
    drains.append(lambda: every(kvpart, kvp_s, kvp_r, {"row": peer(1)}).wait_send())
    qg = nn(sgrad, keys)
    for i in range(heads):
        qg_all[row, :, i * HEAD:(i + 1) * HEAD] = unrotate(qg[i * S:(i + 1) * S]).astype(BF16)
    row_bcast(qg_all.at[row], qg_all, qg_s, qg_r)
    att = nn(narrow, values).astype(BF16)
    for i in range(heads):
        att_all[row, :, i * HEAD:(i + 1) * HEAD] = att[i * S:(i + 1) * S]

    inner = jnp.concatenate(
        [nt(att_all[row], odown_t[...]), nt(qg_all[row], qup[...])], axis=1)
    lown[0] = jnp.where(core == 0, inner[0:B], inner[B:S])
    lown[1] = jnp.where(core == 0, inner[B:S], inner[0:B])
    low_pair = start(remote(lown.at[1], lown.at[2], lowp.at[0], lowp.at[1], sibling))
    kvt_pair.wait_recv()
    other = kvt.at[:, 2 * lax.rem(pair, 2) + core]
    kvt_other = start(remote(other, other, kvt_s.at[2], kvt_r.at[2], sibling))
    kacc = rs_sum(kvpart, kvrx, kvp_s, kvp_r, 2 * HEAD)
    kvg_all[row, :, 0:HEAD] = unrotate(kacc[:, 0:HEAD]).astype(BF16)
    kvg_all[row, :, HEAD:2 * HEAD] = kacc[:, HEAD:2 * HEAD].astype(BF16)
    row_bcast(kvg_all.at[row], kvg_all, kvg_s, kvg_r)
    low_pair.wait_recv()
    lowz[z] = lown[0] + lown[2]
    z_bcast(lowz.at[z], lowz, lowz_s, lowz_r)
    row_bcast(lowx.at[row], lowx, lowx_s, lowx_r)
    row_bcast(att_all.at[row], att_all, att_s, att_r)

    row_recv(qg_all, qg_r, qg_s)
    order = list(reversed(range(REACH)))

    def hop_length(d, ch):
        return REACH if ch == 0 else counts[d] - REACH

    bgroups = [[-d * (t + 1 + (REACH if ch else 0))
                for ch in (1, 0) for d in dirs if t < hop_length(d, ch)] for t in range(REACH)]
    bgroups[REACH - 1].append(0)

    def sliced(ref, group):
        blocks = []
        for o in group:
            for b in range(2):
                r, half = slice_of(o, b)
                blocks.append(ref[r, half * B:(half + 1) * B, :])
        return jnp.concatenate(blocks, axis=0)

    for t in order:
        gq[t, 0:len(bgroups[t]) * S] = nt(sliced(qg_all, bgroups[t]), wq[...])
    z_recv(lowz, lowz_s, lowz_r)
    inner = lowz[0]
    for i in range(1, Z):
        inner = inner + lowz[i]
    low_all[row, core] = inner.astype(BF16)
    row_bcast(low_all.at[row, core], low_all.at[:, core], low_s, low_r)
    row_recv(kvg_all, kvg_r, kvg_s)
    kvt_sib.wait_recv()
    kvt_other.wait_recv()

    def backward(t):
        g = bgroups[t]
        value = gq[t, 0:len(g) * S] + nn(
            sliced(kvg_all, g), kvt[...].reshape(2 * HEAD, D))
        value = value.reshape(len(g), 2, B, D)
        mine = core == 0
        sib_out[t, 0:len(g)] = jnp.where(mine, value[:, 1], value[:, 0]).astype(BF16)
        cp = start(remote(sib_out.at[t, pl.ds(0, len(g))], sib_in.at[t, pl.ds(0, len(g))],
                          sg_s.at[t], sg_r.at[t], sibling))
        own[t, 0:len(g)] = jnp.where(mine, value[:, 0], value[:, 1])
        return cp

    hops = {}

    def hop(d, ch, t):
        i = 0 if d == 1 else 1
        far = ch == 1 and t == REACH - 1
        return remote(hop_out.at[i, ch, t], hop_in.at[i, ch, t], hop_s.at[i, ch, t],
                      hop_r.at[i, ch, t], at_z(z + d * (REACH + 1 if far else 1)))

    def hop_step(t, cp):
        u = REACH - 1 - t
        cp.wait_recv()
        for ch in (1, 0):
            for d in dirs:
                delta = u + 1 + (REACH if ch else 0)
                last = REACH if ch == 0 else counts[d]
                if delta > last:
                    continue
                i = 0 if d == 1 else 1
                slot = bgroups[u].index(d * delta if d * delta in bgroups[u] else -d * delta)
                term = own[u, slot] + sib_in[u, slot].astype(F32)
                if delta < last:
                    hops[d, ch, t - 1].wait_recv()
                    term = term + hop_in[i, ch, t - 1].astype(F32)
                hop_out[i, ch, t] = term.astype(BF16)
                hops[d, ch, t] = start(hop(d, ch, t))

    sibs = {}
    for t, u in enumerate(order):
        sibs[t] = backward(u)
        if t > 0:
            hop_step(t - 1, sibs[t - 1])
    own_slot = bgroups[REACH - 1].index(0)
    final = own[REACH - 1, own_slot] + sib_in[REACH - 1, own_slot].astype(F32)
    low_all_row = low_all.at[:, core]
    row_recv(low_all_row, low_r, low_s)
    low_half = start(remote(low_all_row, low_all_row, lowsib.at[0], lowsib.at[1], sibling))
    hop_step(REACH - 1, sibs[REACH - 1])
    row_recv(lowx, lowx_r, lowx_s)
    lows_all = lowx[...].reshape(T, 128)
    qup_g[...] = 2.0 * tn(lows_all, qg_all[...].reshape(T, H))[RANK:2 * RANK]
    flush()
    low_half.wait_recv()
    for (o, b), (r, half) in slices.items():
        low_nat[o, b] = low_all[r, half]
    lb = low_nat[...].reshape(T, 128)
    oup_g[...] = 2.0 * tn(lb, w_all[...].reshape(T, D))[0:RANK]
    qdown_g[...] = 2.0 * tn(lb, n_all[...].reshape(T, D))[RANK:2 * RANK]
    low_back = low_nat[z, core][:, RANK:2 * RANK]
    final = final + 2.0 * nn(low_back, small[2:4].reshape(RANK, D))
    for ch in (0, 1):
        for d in dirs:
            if hop_length(d, ch) > 0:
                hops[d, ch, REACH - 1].wait_recv()
                final = final + hop_in[0 if d == 1 else 1, ch, REACH - 1].astype(F32)
    dots[row] = jnp.broadcast_to(
        jnp.sum(hf * gf * final, axis=1, keepdims=True), (B, 128))
    row_bcast(dots.at[row], dots, dot_s, dot_r)
    row_recv(att_all, att_r, att_s)
    odown_g[...] = 2.0 * tn(aux_s[...].reshape(T, 128), att_all[...].reshape(T, H))[128 - RANK:128]
    inv = inv_own
    flush()
    base = w_own.astype(F32) + inv * gf * final
    row_recv(dots, dot_r, dot_s)
    dsum = dots[0]
    for i in range(1, R):
        dsum = dsum + dots[i]
    igrad[...] = base - hf * (inv * inv * inv * dsum[:, 0:1] * (1.0 / MODEL_WIDTH))

    flush()


def finish(*refs):
    n = len(refs) // 2
    for i in range(n):
        refs[n + i][...] = refs[i][...]


def per_device(
    hidden, cotangent, importance, positions, segments, norm_gain, query_weight_matrix,
    key_weight, value_weight_matrix, output_weight_matrix, query_down_factor, query_up_factor,
    output_down_factor, out_up,
):
    R = lax.axis_size("row")
    C = lax.axis_size("col")
    Z = C // 2
    B, D = hidden.shape
    H = query_weight_matrix.shape[1]
    S = 2 * B
    CH = Z // REACH
    vmem = pl.BlockSpec(memory_space=pltpu.VMEM)
    dma = pltpu.SemaphoreType.DMA
    outs = (
        jax.ShapeDtypeStruct((B, D), F32),
        jax.ShapeDtypeStruct((RANK, D), F32),
        jax.ShapeDtypeStruct((RANK, H), F32),
        jax.ShapeDtypeStruct((RANK, H), F32),
        jax.ShapeDtypeStruct((RANK, D), F32),
    )
    scratch = [
        pltpu.VMEM((D, H), BF16),
        pltpu.VMEM((H, D), BF16),
        pltpu.VMEM((RANK, D), BF16),
        pltpu.VMEM((RANK, H), BF16),
        pltpu.VMEM((RANK, H), BF16),
        pltpu.VMEM((4, 32, D), BF16),
        pltpu.VMEM((Z, 2, B, D), BF16),
        pltpu.VMEM((Z, 2, B, D), BF16),
        pltpu.VMEM((Z, S, D), BF16),
        pltpu.VMEM((Z, 2, B, 128), BF16),
        pltpu.VMEM((2, GROUP, HEAD // GROUP, D), BF16),
        pltpu.VMEM((R, B, 128), F32),
        pltpu.VMEM((R, 2, B, H), BF16),
        pltpu.VMEM((R, 2, B, H), BF16),
        pltpu.VMEM((R, 2, B, H + 128), BF16),
        pltpu.VMEM((R, 2, B, H + 128), BF16),
        pltpu.VMEM((R, 2, B, 128), BF16),
        pltpu.VMEM((Z, 2, B, 128), BF16),
        pltpu.VMEM((GROUP, S, HEAD), F32),
        pltpu.VMEM((R, S, 2 * HEAD), BF16),
        pltpu.VMEM((R, S, 128), BF16),
        pltpu.VMEM((R, S, 2 * HEAD), BF16),
        pltpu.VMEM((R, S, 2 * HEAD), BF16),
        pltpu.VMEM((R, S, H), BF16),
        pltpu.VMEM((R, S, 2 * HEAD), BF16),
        pltpu.VMEM((R, S, H), BF16),
        pltpu.VMEM((R, B, 128), F32),
        pltpu.VMEM((3, B, 128), F32),
        pltpu.VMEM((Z, B, 128), F32),
        pltpu.VMEM((R, 2, B, 128), BF16),
        pltpu.VMEM((REACH, CH * S, D), F32),
        pltpu.VMEM((REACH, CH, B, D), F32),
        pltpu.VMEM((REACH, CH, B, D), BF16),
        pltpu.VMEM((REACH, CH, B, D), BF16),
        pltpu.VMEM((2, 2, REACH, B, D), BF16),
        pltpu.VMEM((2, 2, REACH, B, D), BF16),
        dma((9,)),
        dma((2, 2, 2, 8)), dma((2, 2, 2, 8)),
        dma((2, 8, 4)), dma((2, 8, 4)),
        dma((1,)), dma((1,)),
        dma((1,)), dma((1,)), dma((2,)),
        dma((3,)), dma((3,)),
        dma((1,)), dma((1,)),
        dma((1,)), dma((1,)),
        dma((3,)), dma((3,)),
        dma((1,)), dma((1,)),
        dma((1,)), dma((1,)),
        dma((1,)), dma((1,)),
        dma((1,)), dma((1,)),
        dma((1,)), dma((1,)),
        dma((1,)), dma((1,)),
        dma((2,)), dma((1,)), dma((1,)),
        dma((1,)), dma((1,)), dma((2,)),
        dma((REACH,)), dma((REACH,)),
        dma((2, 2, REACH)), dma((2, 2, REACH)),
        dma((1,)), dma((1,)),
    ]
    results = pl.pallas_call(
        functools.partial(kernel, R, Z),
        out_shape=outs,
        in_specs=[vmem] * 6 + [pl.BlockSpec(memory_space=pl.ANY)] * 8,
        out_specs=[vmem] * 5,
        scratch_shapes=scratch,
        compiler_params=pltpu.CompilerParams(
            collective_id=0, has_side_effects=True, vmem_limit_bytes=56 * 1024 * 1024),
        name="attention_backward",
    )(
        hidden, cotangent, importance, positions, segments, norm_gain, query_weight_matrix,
        query_down_factor.T, key_weight.T, value_weight_matrix.T, output_weight_matrix, out_up,
        output_down_factor.T, query_up_factor,
    )
    input_grad, qdown_g, qup_g, odown_g, oup_g = pl.pallas_call(
        finish,
        out_shape=outs,
        in_specs=[vmem] * 5,
        out_specs=[vmem] * 5,
        name="place_results",
    )(*results)
    return input_grad, qdown_g.T, qup_g, odown_g.T, oup_g


def solution(mesh):
    placed = (
        P("col", "row"), P("col", "row"), P("col"), P("col"), P("col"), P("row"),
        P("row", "col"), P("row", "col"), P("row", "col"), P("col", "row"),
        P("row", None), P(None, "col"), P("col", None), P(None, "row"),
    )
    return jax.shard_map(
        per_device,
        mesh=mesh,
        in_specs=placed,
        out_specs=(P("col", "row"), P("row", None), P(None, "col"), P("col", None), P(None, "row")),
        check_vma=False,
    )
```

```python
import functools
import math

import jax
import jax.numpy as jnp
from jax import lax
from jax.experimental import pallas as pl
from jax.experimental.pallas import tpu as pltpu
from jax.sharding import PartitionSpec as P

MODEL_WIDTH = 16384
HEAD = 128
RANK = 64
GROUP = 4
EPS = 1e-05
CAP = 2.0
BASE = 500000.0
FILL = -1e30
SCALE = HEAD**-0.5
MESH = pl.DeviceIdType.MESH
F32 = jnp.float32
BF16 = jnp.bfloat16
REACH = 4
NEAR = 4
STEPS = 4
SHIFT = 3


def nn(a, b):
    return lax.dot_general(a, b, (((1,), (0,)), ((), ())), preferred_element_type=F32)


def nt(a, b):
    return lax.dot_general(a, b, (((1,), (1,)), ((), ())), preferred_element_type=F32)


def tn(a, b):
    return lax.dot_general(a, b, (((0,), (0,)), ((), ())), preferred_element_type=F32)


def remote(src, dst, send, recv, device):
    return pltpu.make_async_remote_copy(
        src_ref=src, dst_ref=dst, send_sem=send, recv_sem=recv,
        device_id=device, device_id_type=MESH,
    )


def kernel(
    R, Z,
    hid, cot, imp, posn, segm, gain,
    wq_hbm, qdown_hbm, kw_hbm, vw_hbm, wo_hbm, oup_hbm, odown_hbm, qup_hbm,
    igrad, qdown_g, qup_g, odown_g, oup_g,
    wq, wo, oup, odown_t, qup, small,
    h_all, w_all, n_all, aux_all, kvt,
    ssq, part_w, rx_w, part_h, rx_h, aux_s, low_nat, kvgrp, kvx, lowx, kvpart, kvrx,
    qg_all, kvg_all, att_all, dots,
    lown, lowz, low_all, gq, own, sib_out, sib_in, hop_out, hop_in,
    load, ring_s, ring_r, sib_s, sib_r, ssq_s, ssq_r, auxz_s, auxz_r, auxsib, kvt_s, kvt_r,
    rsw_s, rsw_r, rsh_s, rsh_r, grp_s, grp_r, kvx_s, kvx_r, lowx_s, lowx_r,
    kvp_s, kvp_r, qg_s, qg_r, kvg_s, kvg_r, att_s, att_r,
    lowp, lowz_s, lowz_r, low_s, low_r, lowsib, sg_s, sg_r, hop_s, hop_r, dot_s, dot_r,
):
    row = lax.axis_index("row")
    col = lax.axis_index("col")
    z = lax.div(col, 2)
    core = lax.rem(col, 2)
    B, D = hid.shape
    S = 2 * B
    T = S * Z
    H = wo_hbm.shape[0]
    heads = H // HEAD
    counts = {1: Z // 2, -1: Z - 1 - Z // 2}
    dirs = (1, -1)
    drains = []

    def zmod(v):
        return lax.rem(v + 2 * Z, Z)

    def at_z(v):
        return {"col": zmod(v) * 2 + core}

    sibling = {"col": z * 2 + 1 - core}
    pair = z + 1 - 2 * lax.rem(z, 2)

    def peer(k):
        return lax.rem(row + k, R)

    def each(n, f):
        for k in range(1, n):
            f(k)

    def start(cp):
        cp.start()
        drains.append(cp.wait_send)
        return cp

    def every(ref, ss, rs, device):
        most = ref.at[pl.ds(0, R - 1)]
        return remote(most, most, ss.at[0], rs.at[0], device)

    def row_bcast(src, dst_all, ss, rs):
        each(R, lambda k: remote(
            src, dst_all.at[row], ss.at[0], rs.at[0], {"row": peer(k)}).start())
        drains.append(lambda: every(dst_all, ss, rs, {"row": peer(1)}).wait_send())

    def row_recv(dst_all, rs, ss):
        every(dst_all, ss, rs, {"row": peer(1)}).wait_recv()

    def z_bcast(src, dst_all, ss, rs):
        each(Z, lambda k: remote(
            src, dst_all.at[z], ss.at[0], rs.at[0], at_z(z + k)).start())
        drains.append(lambda: every(dst_all, ss, rs, at_z(z + 1)).wait_send())

    def z_recv(dst_all, ss, rs):
        every(dst_all, ss, rs, at_z(z + 1)).wait_recv()

    loads = {}
    for i, (name, src, dst) in enumerate((
        ("oup", oup_hbm, oup), ("kw", kw_hbm, small.at[0]), ("vw", vw_hbm, small.at[1]),
        ("qd0", qdown_hbm.at[pl.ds(0, 32)], small.at[2]),
        ("qd1", qdown_hbm.at[pl.ds(32, 32)], small.at[3]),
        ("wo", wo_hbm, wo), ("wq", wq_hbm, wq), ("odown", odown_hbm, odown_t),
        ("qup", qup_hbm, qup),
    )):
        loads[name] = pltpu.make_async_copy(src, dst, load.at[i])

    def loaded(*names):
        for name in names:
            loads[name].wait()

    def flush():
        for wait in drains:
            wait()
        drains.clear()

    barrier = pltpu.get_barrier_semaphore()
    each(R, lambda k: pl.semaphore_signal(
        barrier, inc=1, device_id={"row": peer(k)}, device_id_type=MESH))
    each(Z, lambda k: pl.semaphore_signal(
        barrier, inc=1, device_id=at_z(z + k), device_id_type=MESH))
    pl.semaphore_signal(barrier, inc=1, device_id=sibling, device_id_type=MESH)
    pl.semaphore_signal(
        barrier, inc=1, device_id={"col": pair * 2 + 1 - core}, device_id_type=MESH)
    for cp in loads.values():
        cp.start()

    diagonal = (lax.broadcasted_iota(jnp.int32, (B, B), 0)
                == lax.broadcasted_iota(jnp.int32, (B, B), 1))

    def column(v):
        return jnp.sum(jnp.where(diagonal, v.reshape(1, B), 0.0), axis=1, keepdims=True)

    hf = hid[...].astype(F32)
    gf = gain[...].astype(F32).reshape(1, D)
    w_own = (cot[...].astype(F32)
             * column(jnp.minimum(imp[...].astype(F32), CAP))).astype(BF16)
    w_all[z, core] = w_own
    h_all[z, core] = hid[...]
    loaded("oup")
    ssq[row] = jnp.concatenate([
        jnp.broadcast_to(jnp.sum(hf * hf, axis=1, keepdims=True), (B, 128 - RANK)),
        nt(w_own, oup[...])], axis=1)
    member = lax.rem(col, GROUP)
    pl.semaphore_wait(barrier, R - 1 + Z - 1 + 2)

    arrays = (h_all, w_all)

    def length(d, ch):
        return NEAR if ch == 0 else counts[d] - NEAR

    def ring_send(a, d, ch, t):
        off = t if ch == 0 else (0 if t == 0 else NEAR + t)
        block = arrays[a].at[zmod(z - d * off), core]
        target = z + d * (NEAR + 1 if ch == 1 and t == 0 else 1)
        i = 0 if d == 1 else 1
        return start(remote(
            block, block, ring_s.at[a, i, ch, t], ring_r.at[a, i, ch, t], at_z(target)))

    halves = {}

    def sib_send(a, t, i, off):
        block = arrays[a].at[zmod(z + off), core]
        cp = start(remote(block, block, sib_s.at[a, t, i], sib_r.at[a, t, i], sibling))
        halves.setdefault((a, min(t, STEPS - 1)), []).append(cp)

    flying = {}
    for ch in (0, 1):
        for a in range(2):
            for d in dirs:
                if length(d, ch) > 0:
                    flying[a, d, ch] = ring_send(a, d, ch, 0)
    row_bcast(ssq.at[row], ssq, ssq_s, ssq_r)
    for a in range(2):
        sib_send(a, STEPS, 3, 0)

    def ring_part(t, ch):
        came = []
        for a in range(2):
            for i, d in enumerate(dirs):
                if t >= length(d, ch):
                    continue
                flying[a, d, ch].wait_recv()
                if t + 1 < length(d, ch):
                    flying[a, d, ch] = ring_send(a, d, ch, t + 1)
                came.append((a, t, 2 * ch + i, -d * (t + 1 + (NEAR if ch else 0))))
        for arrival in came:
            sib_send(*arrival)

    def ring_step(t):
        ring_part(t, 0)
        ring_part(t, 1)

    def chips_of(t):
        return [-d * (t + 1 + (NEAR if ch else 0))
                for ch in (1, 0) for d in dirs if t < length(d, ch)]

    groups = [chips_of(t) for t in range(STEPS - 1)]
    groups.append(chips_of(STEPS - 1) + chips_of(STEPS) + [0])

    def slice_of(o, b):
        return zmod(z + o + SHIFT * b), b

    slices = {(c, b): ((c + SHIFT * b) % Z, b) for c in range(Z) for b in range(2)}

    ring_part(0, 0)
    row_recv(ssq, ssq_r, ssq_s)
    total = ssq[0]
    for i in range(1, R):
        total = total + ssq[i]
    inv_own = lax.rsqrt(total[:, 0:1] * (1.0 / MODEL_WIDTH) + EPS)
    lane = lax.broadcasted_iota(jnp.int32, (B, 128), 1)
    hi = inv_own.astype(BF16).astype(F32)
    mid = (inv_own - hi).astype(BF16).astype(F32)
    lo = inv_own - hi - mid
    p_own = posn[...]
    p_hi = lax.div(p_own, 64)
    tile = jnp.where(lane >= 128 - RANK, total, jnp.where(lane == 0, hi, jnp.where(
        lane == 1, mid, lo)))
    for i, v in ((3, p_hi), (4, p_own - p_hi * 64), (5, segm[...])):
        tile = jnp.where(lane == i, column(v.astype(F32)), tile)
    tile = jnp.where(lane == 6, col.astype(F32), tile)
    tile = jnp.where(
        lane == 7, lax.broadcasted_iota(jnp.int32, (B, 128), 0).astype(F32), tile)
    aux_all[z, core] = tile.astype(BF16)
    z_bcast(aux_all.at[z, core], aux_all.at[:, core], auxz_s, auxz_r)
    ring_part(0, 1)

    def rs_send(gi, src, dst, ss, rs):
        for b in range(2):
            for o in groups[gi]:
                p = zmod(z + o + SHIFT * b)

                @pl.when(p != row)
                def _():
                    remote(src.at[p, b], dst.at[row, b], ss.at[0], rs.at[0], {"row": p}).start()

    def rs_drain(src, ss, rs):
        drains.append(lambda: every(src, ss, rs, {"row": peer(1)}).wait_send())

    def rows_of(ref, group, width):
        return jnp.concatenate(
            [ref[zmod(z + o)].reshape(S, width) for o in group], axis=0)

    def store(ref, group, value, at):
        for i, o in enumerate(group):
            for b in range(2):
                r, half = slice_of(o, b)
                ref[r, half, :, at] = value[i * S + b * B:i * S + (b + 1) * B]

    def project_w(t):
        g = groups[t]
        for cp in halves[1, t]:
            cp.wait_recv()
        store(part_w, g, nt(rows_of(w_all, g, D), wo[...]).astype(BF16), slice(0, H))
        rs_send(t, part_w, rx_w, rsw_s, rsw_r)

    def project_h(t):
        g = groups[t]
        for cp in halves[0, t]:
            cp.wait_recv()
        ax = rows_of(aux_all, g, 128).astype(F32)
        h = rows_of(h_all, g, D).astype(F32)
        n = (h * (ax[:, 0:1] + ax[:, 1:2] + ax[:, 2:3]) * gf).astype(BF16)
        for i, o in enumerate(g):
            n_all[zmod(z + o)] = n[i * S:(i + 1) * S]
        store(part_h, g, nt(n, small[...].reshape(128, D)).astype(BF16), slice(H, H + 128))
        store(part_h, g, nn(n, wq[...]).astype(BF16), slice(0, H))
        rs_send(t, part_h, rx_h, rsh_s, rsh_r)

    ring_step(1)
    loaded("wo")
    project_w(0)
    ring_step(2)
    z_recv(aux_all.at[:, core], auxz_s, auxz_r)
    aux_half = start(remote(
        aux_all.at[:, core], aux_all.at[:, core], auxsib.at[0], auxsib.at[1], sibling))
    project_w(1)
    loaded("kw", "vw", "qd0", "qd1", "wq")
    aux_half.wait_recv()
    project_h(0)
    ring_step(3)
    project_h(1)
    project_w(2)
    ring_step(4)
    project_h(2)
    project_h(3)
    project_w(3)
    kvt[:, member] = small[0:2]
    kvt_own = kvt.at[:, member]
    kvt_sib = start(remote(kvt_own, kvt_own, kvt_s.at[0], kvt_r.at[0], sibling))
    kvt_pair = start(remote(
        kvt_own, kvt_own, kvt_s.at[1], kvt_r.at[1], {"col": pair * 2 + core}))
    rs_drain(part_w, rsw_s, rsw_r)
    rs_drain(part_h, rsh_s, rsh_r)

    for (o, b), (r, half) in slices.items():
        aux_s[r, half] = aux_all[o, b]
    ax = aux_s[row].reshape(S, 128).astype(F32)
    pos = ax[:, 3:4] * 64.0 + ax[:, 4:5]
    lane_s = lax.broadcasted_iota(jnp.int32, (S, HEAD), 1)
    half_lane = lax.rem(lane_s, HEAD // 2).astype(F32)
    angle = pos * jnp.exp(half_lane * (-2.0 * math.log(BASE) / HEAD))
    cosine = jnp.cos(angle)
    sine = jnp.where(lane_s < HEAD // 2, -1.0, 1.0) * jnp.sin(angle)

    def swap(x):
        return jnp.concatenate([x[:, HEAD // 2:], x[:, :HEAD // 2]], axis=1)

    def rotate(x):
        return x * cosine + swap(x) * sine

    def unrotate(x):
        return x * cosine - swap(x) * sine

    pick_row = lax.broadcasted_iota(jnp.int32, (8, 128), 0)
    pick_lane = lax.broadcasted_iota(jnp.int32, (8, 128), 1)
    pick = jnp.where(pick_row == 0, (pick_lane == 5).astype(F32), jnp.where(
        pick_row == 1, jnp.where(pick_lane == 6, float(B), (pick_lane == 7).astype(F32)), 0.0))
    of_key = nt(pick.astype(BF16), aux_s[...].reshape(T, 128))
    token = ax[:, 6:7] * float(B) + ax[:, 7:8]
    allowed = (ax[:, 5:6] == of_key[0:1, :]) & (of_key[1:2, :] <= token)
    allowed = jnp.concatenate([allowed.astype(F32)] * heads, axis=0) > 0.5

    def rs_sum(part, rx, ss, rs, width):
        row_recv(rx, rs, ss)
        acc = part[row].reshape(S, width).astype(F32)
        for k in range(1, R):
            acc = acc + rx[peer(k)].reshape(S, width).astype(F32)
        return acc

    summed = rs_sum(part_h, rx_h, rsh_s, rsh_r, H + 128)
    kvl = summed[:, H:H + 128]
    kvgrp[member] = kvl
    kvl_cp = []
    for i, dev in enumerate((sibling, {"col": pair * 2 + core}, {"col": pair * 2 + 1 - core})):
        kvl_cp.append(start(remote(
            kvgrp.at[member], kvgrp.at[member], grp_s.at[i], grp_r.at[i], dev)))
    low = kvl.astype(BF16)
    lowx[row] = low
    loaded("qup", "odown")
    ql = 2.0 * nn(low[:, RANK:2 * RANK], qup[...])
    dA = 2.0 * nn(aux_s[row].reshape(S, 128)[:, 128 - RANK:128], odown_t[...])
    for cp in kvl_cp:
        cp.wait_recv()
    part = HEAD // GROUP
    kl, vl = (jnp.concatenate(
        [kvgrp[g][:, half * part:(half + 1) * part] for g in range(GROUP)], axis=1)
        for half in range(2))
    kvx[row, :, 0:HEAD] = rotate(kl).astype(BF16)
    kvx[row, :, HEAD:2 * HEAD] = vl.astype(BF16)
    row_bcast(kvx.at[row], kvx, kvx_s, kvx_r)
    ql = ql + summed[:, 0:H]
    queries = jnp.concatenate(
        [rotate(ql[:, i * HEAD:(i + 1) * HEAD]).astype(BF16) for i in range(heads)], axis=0)
    row_recv(kvx, kvx_r, kvx_s)

    keys = kvx[:, :, 0:HEAD].reshape(T, HEAD)
    values = kvx[:, :, HEAD:2 * HEAD].reshape(T, HEAD)
    scores = jnp.where(allowed, nt(queries, keys) * SCALE, FILL)
    shifted = jnp.exp(scores - jnp.max(scores, axis=1, keepdims=True))
    probs = shifted / jnp.sum(shifted, axis=1, keepdims=True)
    narrow = probs.astype(BF16)
    dA = (dA + rs_sum(part_w, rx_w, rsw_s, rsw_r, H)).astype(BF16)
    grads = jnp.concatenate([dA[:, i * HEAD:(i + 1) * HEAD] for i in range(heads)], axis=0)
    pgrad = nt(grads, values)
    rdot = jnp.sum(probs * pgrad, axis=1, keepdims=True)
    sgrad = (probs * (pgrad - rdot) * SCALE).astype(BF16)
    kvpart[:, :, 0:HEAD] = tn(sgrad, queries).astype(BF16).reshape(R, S, HEAD)
    kvpart[:, :, HEAD:2 * HEAD] = tn(narrow, grads).astype(BF16).reshape(R, S, HEAD)

    each(R, lambda k: remote(
        kvpart.at[peer(k)], kvrx.at[row], kvp_s.at[0], kvp_r.at[0], {"row": peer(k)}).start())
    drains.append(lambda: every(kvpart, kvp_s, kvp_r, {"row": peer(1)}).wait_send())
    qg = nn(sgrad, keys)
    for i in range(heads):
        qg_all[row, :, i * HEAD:(i + 1) * HEAD] = unrotate(qg[i * S:(i + 1) * S]).astype(BF16)
    att = nn(narrow, values).astype(BF16)
    for i in range(heads):
        att_all[row, :, i * HEAD:(i + 1) * HEAD] = att[i * S:(i + 1) * S]

    inner = jnp.concatenate(
        [nt(att_all[row], odown_t[...]), nt(qg_all[row], qup[...])], axis=1)
    lown[0] = jnp.where(core == 0, inner[0:B], inner[B:S])
    lown[1] = jnp.where(core == 0, inner[B:S], inner[0:B])
    low_pair = start(remote(lown.at[1], lown.at[2], lowp.at[0], lowp.at[1], sibling))
    kvt_pair.wait_recv()
    other = kvt.at[:, 2 * lax.rem(pair, 2) + core]
    kvt_other = start(remote(other, other, kvt_s.at[2], kvt_r.at[2], sibling))
    kacc = rs_sum(kvpart, kvrx, kvp_s, kvp_r, 2 * HEAD)
    kvg_all[row, :, 0:HEAD] = unrotate(kacc[:, 0:HEAD]).astype(BF16)
    kvg_all[row, :, HEAD:2 * HEAD] = kacc[:, HEAD:2 * HEAD].astype(BF16)
    row_bcast(kvg_all.at[row], kvg_all, kvg_s, kvg_r)
    row_bcast(qg_all.at[row], qg_all, qg_s, qg_r)
    low_pair.wait_recv()
    lowz[z] = lown[0] + lown[2]
    z_bcast(lowz.at[z], lowz, lowz_s, lowz_r)

    row_recv(qg_all, qg_r, qg_s)
    order = list(reversed(range(REACH)))

    def hop_length(d, ch):
        return REACH if ch == 0 else counts[d] - REACH

    bgroups = [[-d * (t + 1 + (REACH if ch else 0))
                for ch in (1, 0) for d in dirs if t < hop_length(d, ch)] for t in range(REACH)]
    bgroups[REACH - 1].append(0)

    def sliced(ref, group):
        blocks = []
        for o in group:
            for b in range(2):
                r, half = slice_of(o, b)
                blocks.append(ref[r, half * B:(half + 1) * B, :])
        return jnp.concatenate(blocks, axis=0)

    for t in order:
        gq[t, 0:len(bgroups[t]) * S] = nt(sliced(qg_all, bgroups[t]), wq[...])
    z_recv(lowz, lowz_s, lowz_r)
    inner = lowz[0]
    for i in range(1, Z):
        inner = inner + lowz[i]
    low_all[row, core] = inner.astype(BF16)
    row_bcast(low_all.at[row, core], low_all.at[:, core], low_s, low_r)
    row_recv(kvg_all, kvg_r, kvg_s)
    row_bcast(lowx.at[row], lowx, lowx_s, lowx_r)
    row_bcast(att_all.at[row], att_all, att_s, att_r)
    kvt_sib.wait_recv()
    kvt_other.wait_recv()

    def backward(t):
        g = bgroups[t]
        value = gq[t, 0:len(g) * S] + nn(
            sliced(kvg_all, g), kvt[...].reshape(2 * HEAD, D))
        value = value.reshape(len(g), 2, B, D)
        mine = core == 0
        sib_out[t, 0:len(g)] = jnp.where(mine, value[:, 1], value[:, 0]).astype(BF16)
        cp = start(remote(sib_out.at[t, pl.ds(0, len(g))], sib_in.at[t, pl.ds(0, len(g))],
                          sg_s.at[t], sg_r.at[t], sibling))
        own[t, 0:len(g)] = jnp.where(mine, value[:, 0], value[:, 1])
        return cp

    hops = {}

    def hop(d, ch, t):
        i = 0 if d == 1 else 1
        far = ch == 1 and t == REACH - 1
        return remote(hop_out.at[i, ch, t], hop_in.at[i, ch, t], hop_s.at[i, ch, t],
                      hop_r.at[i, ch, t], at_z(z + d * (REACH + 1 if far else 1)))

    def hop_step(t, cp):
        u = REACH - 1 - t
        cp.wait_recv()
        for ch in (1, 0):
            for d in dirs:
                delta = u + 1 + (REACH if ch else 0)
                last = REACH if ch == 0 else counts[d]
                if delta > last:
                    continue
                i = 0 if d == 1 else 1
                slot = bgroups[u].index(d * delta if d * delta in bgroups[u] else -d * delta)
                term = own[u, slot] + sib_in[u, slot].astype(F32)
                if delta < last:
                    hops[d, ch, t - 1].wait_recv()
                    term = term + hop_in[i, ch, t - 1].astype(F32)
                hop_out[i, ch, t] = term.astype(BF16)
                hops[d, ch, t] = start(hop(d, ch, t))

    sibs = {}
    for t, u in enumerate(order):
        sibs[t] = backward(u)
        if t > 0:
            hop_step(t - 1, sibs[t - 1])
    own_slot = bgroups[REACH - 1].index(0)
    final = own[REACH - 1, own_slot] + sib_in[REACH - 1, own_slot].astype(F32)
    low_all_row = low_all.at[:, core]
    row_recv(low_all_row, low_r, low_s)
    low_half = start(remote(low_all_row, low_all_row, lowsib.at[0], lowsib.at[1], sibling))
    hop_step(REACH - 1, sibs[REACH - 1])
    row_recv(lowx, lowx_r, lowx_s)
    lows_all = lowx[...].reshape(T, 128)
    qup_g[...] = 2.0 * tn(lows_all, qg_all[...].reshape(T, H))[RANK:2 * RANK]
    flush()
    low_half.wait_recv()
    for (o, b), (r, half) in slices.items():
        low_nat[o, b] = low_all[r, half]
    lb = low_nat[...].reshape(T, 128)
    oup_g[...] = 2.0 * tn(lb, w_all[...].reshape(T, D))[0:RANK]
    qdown_g[...] = 2.0 * tn(lb, n_all[...].reshape(T, D))[RANK:2 * RANK]
    low_back = low_nat[z, core][:, RANK:2 * RANK]
    final = final + 2.0 * nn(low_back, small[2:4].reshape(RANK, D))
    for ch in (0, 1):
        for d in dirs:
            if hop_length(d, ch) > 0:
                hops[d, ch, REACH - 1].wait_recv()
                final = final + hop_in[0 if d == 1 else 1, ch, REACH - 1].astype(F32)
    dots[row] = jnp.broadcast_to(
        jnp.sum(hf * gf * final, axis=1, keepdims=True), (B, 128))
    row_bcast(dots.at[row], dots, dot_s, dot_r)
    row_recv(att_all, att_r, att_s)
    odown_g[...] = 2.0 * tn(aux_s[...].reshape(T, 128), att_all[...].reshape(T, H))[128 - RANK:128]
    inv = inv_own
    flush()
    base = w_own.astype(F32) + inv * gf * final
    row_recv(dots, dot_r, dot_s)
    dsum = dots[0]
    for i in range(1, R):
        dsum = dsum + dots[i]
    igrad[...] = base - hf * (inv * inv * inv * dsum[:, 0:1] * (1.0 / MODEL_WIDTH))

    flush()


def finish(*refs):
    n = len(refs) // 2
    for i in range(n):
        refs[n + i][...] = refs[i][...]


def per_device(
    hidden, cotangent, importance, positions, segments, norm_gain, query_weight_matrix,
    key_weight, value_weight_matrix, output_weight_matrix, query_down_factor, query_up_factor,
    output_down_factor, out_up,
):
    R = lax.axis_size("row")
    C = lax.axis_size("col")
    Z = C // 2
    B, D = hidden.shape
    H = query_weight_matrix.shape[1]
    S = 2 * B
    CH = Z // REACH
    vmem = pl.BlockSpec(memory_space=pltpu.VMEM)
    dma = pltpu.SemaphoreType.DMA
    outs = (
        jax.ShapeDtypeStruct((B, D), F32),
        jax.ShapeDtypeStruct((RANK, D), F32),
        jax.ShapeDtypeStruct((RANK, H), F32),
        jax.ShapeDtypeStruct((RANK, H), F32),
        jax.ShapeDtypeStruct((RANK, D), F32),
    )
    scratch = [
        pltpu.VMEM((D, H), BF16),
        pltpu.VMEM((H, D), BF16),
        pltpu.VMEM((RANK, D), BF16),
        pltpu.VMEM((RANK, H), BF16),
        pltpu.VMEM((RANK, H), BF16),
        pltpu.VMEM((4, 32, D), BF16),
        pltpu.VMEM((Z, 2, B, D), BF16),
        pltpu.VMEM((Z, 2, B, D), BF16),
        pltpu.VMEM((Z, S, D), BF16),
        pltpu.VMEM((Z, 2, B, 128), BF16),
        pltpu.VMEM((2, GROUP, HEAD // GROUP, D), BF16),
        pltpu.VMEM((R, B, 128), F32),
        pltpu.VMEM((R, 2, B, H), BF16),
        pltpu.VMEM((R, 2, B, H), BF16),
        pltpu.VMEM((R, 2, B, H + 128), BF16),
        pltpu.VMEM((R, 2, B, H + 128), BF16),
        pltpu.VMEM((R, 2, B, 128), BF16),
        pltpu.VMEM((Z, 2, B, 128), BF16),
        pltpu.VMEM((GROUP, S, HEAD), F32),
        pltpu.VMEM((R, S, 2 * HEAD), BF16),
        pltpu.VMEM((R, S, 128), BF16),
        pltpu.VMEM((R, S, 2 * HEAD), BF16),
        pltpu.VMEM((R, S, 2 * HEAD), BF16),
        pltpu.VMEM((R, S, H), BF16),
        pltpu.VMEM((R, S, 2 * HEAD), BF16),
        pltpu.VMEM((R, S, H), BF16),
        pltpu.VMEM((R, B, 128), F32),
        pltpu.VMEM((3, B, 128), F32),
        pltpu.VMEM((Z, B, 128), F32),
        pltpu.VMEM((R, 2, B, 128), BF16),
        pltpu.VMEM((REACH, CH * S, D), F32),
        pltpu.VMEM((REACH, CH, B, D), F32),
        pltpu.VMEM((REACH, CH, B, D), BF16),
        pltpu.VMEM((REACH, CH, B, D), BF16),
        pltpu.VMEM((2, 2, REACH, B, D), BF16),
        pltpu.VMEM((2, 2, REACH, B, D), BF16),
        dma((9,)),
        dma((2, 2, 2, 8)), dma((2, 2, 2, 8)),
        dma((2, 8, 4)), dma((2, 8, 4)),
        dma((1,)), dma((1,)),
        dma((1,)), dma((1,)), dma((2,)),
        dma((3,)), dma((3,)),
        dma((1,)), dma((1,)),
        dma((1,)), dma((1,)),
        dma((3,)), dma((3,)),
        dma((1,)), dma((1,)),
        dma((1,)), dma((1,)),
        dma((1,)), dma((1,)),
        dma((1,)), dma((1,)),
        dma((1,)), dma((1,)),
        dma((1,)), dma((1,)),
        dma((2,)), dma((1,)), dma((1,)),
        dma((1,)), dma((1,)), dma((2,)),
        dma((REACH,)), dma((REACH,)),
        dma((2, 2, REACH)), dma((2, 2, REACH)),
        dma((1,)), dma((1,)),
    ]
    results = pl.pallas_call(
        functools.partial(kernel, R, Z),
        out_shape=outs,
        in_specs=[vmem] * 6 + [pl.BlockSpec(memory_space=pl.ANY)] * 8,
        out_specs=[vmem] * 5,
        scratch_shapes=scratch,
        compiler_params=pltpu.CompilerParams(
            collective_id=0, has_side_effects=True, vmem_limit_bytes=56 * 1024 * 1024),
        name="attention_backward",
    )(
        hidden, cotangent, importance, positions, segments, norm_gain, query_weight_matrix,
        query_down_factor.T, key_weight.T, value_weight_matrix.T, output_weight_matrix, out_up,
        output_down_factor.T, query_up_factor,
    )
    input_grad, qdown_g, qup_g, odown_g, oup_g = pl.pallas_call(
        finish,
        out_shape=outs,
        in_specs=[vmem] * 5,
        out_specs=[vmem] * 5,
        name="place_results",
    )(*results)
    return input_grad, qdown_g.T, qup_g, odown_g.T, oup_g


def solution(mesh):
    placed = (
        P("col", "row"), P("col", "row"), P("col"), P("col"), P("col"), P("row"),
        P("row", "col"), P("row", "col"), P("row", "col"), P("col", "row"),
        P("row", None), P(None, "col"), P("col", None), P(None, "row"),
    )
    return jax.shard_map(
        per_device,
        mesh=mesh,
        in_specs=placed,
        out_specs=(P("col", "row"), P("row", None), P(None, "col"), P("col", None), P(None, "row")),
        check_vma=False,
    )
```
